128 devices in a mesh: sec: 4 (over x), tile: 32 (over y, z, core).
Axes of the slice: x: 4, y: 4, z: 4, core: 2. Of those that a mesh axis runs over, the one named last changes fastest.
Arguments:
- strips: bfloat16 [4, 512, 256, 256], P('sec', 'tile'), may hold values from -6 to 6
- partner_tile: int32 [4, 512], P('sec'), may hold values from 0 to 31, as said below
- partner_strip: int32 [4, 512], P('sec'), may hold values from 0 to 15
- adjacency: int32 [6, 4, 512], P(None, 'sec', 'tile'), may hold values from 0 to 511
- start_positions: float32 [2, 4, 512], P(None, 'sec', 'tile'), may hold values from -6 to 6
Outputs:
- plane_flow: float32 [2, 4, 512], P(None, 'sec', 'tile')
- depth_flow: float32 [2, 4, 512], P(None, 'sec', 'tile')
- node_positions: float32 [2, 4, 512], P(None, 'sec', 'tile')
The draws below stay inside these ranges and needn't reach their ends.
Inputs may be any that keep to these rules, and one draw needn't show every extreme that they name: `partner_tile`: within a section, the 16 strips of any one tile name any one tile at most 2 times, and some tile is named exactly 2 times by the strips of every tile.
All inputs are finite; a program needn't handle non-finite values.
Results may differ from the reference program's by a relative error of at most 0.024.
Values may be sent and summed in bfloat16 or wider, within the bound.
No kernel may reach another device: no remote copies, remote signals or barrier semaphores. Data moves between devices by JAX's collectives and lax.ppermute only.
A program may use at most 192 MiB of HBM per device.

```python
import math
import jax
import jax.numpy as jnp
from jax import lax

PATCH = 256
NS = 16
K = 6
STEPS = 2
SEC = 4
NODES = 512
CAP = 2
N_TILE = 32


def section_tiles(key):
    label_key, order_key = jax.random.split(key)
    labels = jax.random.permutation(label_key, N_TILE).astype(jnp.int32)
    positions = jnp.arange(N_TILE * NS, dtype=jnp.int32)
    ranked = positions // (N_TILE * CAP)
    targets = jnp.take(labels, ranked)
    grid = targets.reshape(NS, N_TILE).T
    order_keys = jax.random.split(order_key, N_TILE)
    orders = jax.vmap(lambda single: jax.random.permutation(single, NS))(order_keys).astype(jnp.int32)
    shuffled = jnp.take_along_axis(grid, orders, axis=1)
    return shuffled.reshape(-1).astype(jnp.int32)


def draw_partner_tile(key, part):
    key = jax.random.fold_in(key, 11)
    section_keys = jax.random.split(key, SEC)
    return jax.vmap(section_tiles)(section_keys).astype(jnp.int32)


def touch_ends(values, own_key, least, high):
    shape = values.shape
    place = [jax.random.randint(jax.random.fold_in(own_key, axis), (), 0, shape[axis]) for axis in range(len(shape))]
    values = values.at[tuple(place)].set(least)
    longest = shape.index(max(shape))
    place[longest] = (place[longest] + 1) % shape[longest]
    return values.at[tuple(place)].set(high)


def block_levels(rng, extent, cuts, smallest, top_value):
    level, own = 1.0, jax.random.fold_in(rng, 6)
    for dim, parts in cuts:
        heights = jnp.exp(jax.random.uniform(jax.random.fold_in(own, dim), (parts,), jnp.float32, smallest / len(cuts), top_value / len(cuts)))
        level = level * jnp.repeat(heights, extent[dim] // parts).reshape([-1 if axis == dim else 1 for axis in range(len(extent))])
    return level


def gaussian(rng, shape, deviation, limit, cuts=(), kind=jnp.bfloat16):
    result = deviation * jax.random.normal(rng, shape, jnp.float32)
    if cuts:
        result = result * block_levels(rng, shape, cuts, -0.22, 0.18)
    return jnp.clip(result, -limit, limit).astype(kind)


def setup_inputs(seed: int = 0) -> dict:
    keys = jax.random.split(jax.random.key(seed), 6)
    strips = gaussian(keys[0], (SEC, NODES, PATCH, PATCH), 1.0, 6.0, ((0, 4), (1, 32)))
    partner_tile = draw_partner_tile(jax.random.fold_in(keys[5], 71), 0)
    partner_strip = touch_ends(jax.random.randint(keys[2], (SEC, NODES), 0, NS), jax.random.fold_in(keys[2], 1), 0, NS - 1).astype(jnp.int32)
    adjacency = touch_ends(jax.random.randint(keys[3], (K, SEC, NODES), 0, NODES), jax.random.fold_in(keys[3], 1), 0, NODES - 1).astype(jnp.int32)
    start_positions = gaussian(keys[4], (2, SEC, NODES), 1.0, 6.0, ((1, 4), (2, 32)), jnp.float32)
    return {"strips": strips, "partner_tile": partner_tile, "partner_strip": partner_strip, "adjacency": adjacency, "start_positions": start_positions}


epsilon = 1e-6
relax_rate = 0.1


def dft_spectra(block):
    transform = jnp.fft.fft2(block.astype(jnp.float32))
    return jnp.stack([jnp.real(transform), jnp.imag(transform)], 1).astype(jnp.bfloat16)


def pair_flows(first, second):
    length = first.shape[-1]
    first_re = first[:, 0].astype(jnp.float32)
    first_im = first[:, 1].astype(jnp.float32)
    second_re = second[:, 0].astype(jnp.float32)
    second_im = second[:, 1].astype(jnp.float32)
    cross_re = (first_re * second_re + first_im * second_im).astype(jnp.bfloat16)
    cross_im = (first_re * second_im - first_im * second_re).astype(jnp.bfloat16)
    cross_re, cross_im = lax.optimization_barrier((cross_re, cross_im))
    joined = lax.complex(cross_re.astype(jnp.float32), cross_im.astype(jnp.float32))
    surface = jnp.real(jnp.fft.ifft2(joined)) * (length * length)
    weights = surface * surface
    offsets = (((jnp.arange(length, dtype=jnp.int32) + length // 2) % length) - length // 2).astype(jnp.float32)
    total = jnp.mean(weights, axis=(1, 2)) + epsilon
    along_rows = jnp.mean(weights * offsets[None, :, None], axis=(1, 2)) / total
    along_cols = jnp.mean(weights * offsets[None, None, :], axis=(1, 2)) / total
    return jnp.stack([along_rows, along_cols], 0)


def reference(strips, partner_tile, partner_strip, adjacency, start_positions):
    spectra = lax.map(dft_spectra, strips)
    order = jnp.arange(SEC, dtype=jnp.int32)
    nearby = ((order + 1) % SEC).astype(jnp.int32)
    partner_global = (partner_tile * NS + partner_strip).astype(jnp.int32)
    block = math.gcd(NODES, 64)

    def split_nodes(values):
        return values.reshape((NODES // block, block) + values.shape[1:])

    def per_block(operands):
        first_plane, first_depth, second = operands
        return pair_flows(first_plane, second), pair_flows(first_depth, second)

    def per_section(index):
        own_spectra = lax.dynamic_index_in_dim(spectra, index, 0, keepdims=False)
        near_index = lax.dynamic_index_in_dim(nearby, index, 0, keepdims=False)
        near_spectra = lax.dynamic_index_in_dim(spectra, near_index, 0, keepdims=False)
        partner_row = lax.dynamic_index_in_dim(partner_global, index, 0, keepdims=False)
        partners = jnp.take(own_spectra, partner_row, axis=0)
        plane, depth = lax.map(per_block, (split_nodes(partners), split_nodes(near_spectra), split_nodes(own_spectra)))
        plane = jnp.transpose(plane, (1, 0, 2)).reshape(2, NODES)
        depth = jnp.transpose(depth, (1, 0, 2)).reshape(2, NODES)
        return plane, depth

    plane_all, depth_all = lax.map(per_section, order)
    plane_flow = jnp.transpose(plane_all, (1, 0, 2))
    depth_flow = jnp.transpose(depth_all, (1, 0, 2))
    positions = start_positions
    for iteration in range(STEPS):
        near_nodes = positions[:, nearby, :]
        linked = jnp.stack([jnp.take_along_axis(positions, adjacency[index][None], axis=2) for index in range(K)], 1)
        springs = jnp.sum(linked, axis=1) - K * positions
        partner_nodes = jnp.take_along_axis(positions, partner_global[None], axis=2)
        force = springs + (partner_nodes + plane_flow - positions) + (near_nodes + depth_flow - positions)
        positions = positions + relax_rate * force
    return plane_flow, depth_flow, positions
```

```python
import functools
import math

import jax
import jax.numpy as jnp
import numpy as np
from jax import lax
from jax.experimental import pallas as pl
from jax.experimental.pallas import tpu as pltpu
from jax.sharding import PartitionSpec as P

STEPS = 2


epsilon = 1e-06
relax_rate = 0.1


def shifted(x, axis, by):
    devices = lax.axis_size(axis)
    return lax.ppermute(x, axis, [(i, (i + by) % devices) for i in range(devices)])


def offsets_of(length):
    return ((np.arange(length) + length // 2) % length - length // 2).astype(np.float32)


def angles_of(length):
    indices = np.arange(length)
    return (indices[:, None] * indices[None, :] % length) * (2.0 * math.pi / length)


def half_tables(length):
    half = length // 2
    cosine, sine = np.cos(angles_of(length)), np.sin(angles_of(length))
    to_half = np.concatenate([cosine[:, :half], -sine[:, :half]], 1)
    to_half[:, half] = cosine[:, half]
    from_half = np.concatenate([2.0 * cosine[:half], -2.0 * sine[:half]], 0)
    from_half[0] = 1.0
    from_half[half] = cosine[half]
    both = np.concatenate([cosine, sine], 0)
    return tuple(jnp.asarray(table, jnp.bfloat16) for table in (to_half, both, from_half))


def dot(left, right):
    return jnp.dot(left, right, preferred_element_type=jnp.float32)


def spectrum_fields(image, to_half, both):
    length = image.shape[0]
    half = length // 2
    rows = dot(image, to_half).astype(jnp.bfloat16)
    mixed = dot(both, rows)
    cos_re, cos_im = mixed[:length, :half], mixed[:length, half:]
    sin_re, sin_im = mixed[length:, :half], mixed[length:, half:]
    first = lax.broadcasted_iota(jnp.int32, cos_re.shape, 1) == 0
    fields = (
        jnp.where(first, cos_re, cos_re + sin_im),
        jnp.where(first, sin_re, sin_re - cos_im),
        jnp.where(first, cos_im, 0.0),
        jnp.where(first, sin_im, 0.0),
    )
    return tuple(field.astype(jnp.bfloat16).astype(jnp.float32) for field in fields)


def cross_of(a, b):
    real = a[0] * b[0] + a[1] * b[1] + a[2] * b[3] - a[3] * b[2]
    imag = a[1] * b[0] - a[0] * b[1] + a[2] * b[2] + a[3] * b[3]
    return real.astype(jnp.bfloat16), imag.astype(jnp.bfloat16)


def pair_kernel(first_ref, second_ref, to_half_ref, both_ref, from_half_ref, offsets_ref, out_ref):
    length = first_ref.shape[-1]
    half = length // 2
    to_half, both = to_half_ref[...], both_ref[...]
    first = spectrum_fields(first_ref[0], to_half, both)
    second = spectrum_fields(second_ref[0], to_half, both)
    cross = jnp.concatenate(cross_of(first, second), 1)
    mixed = dot(both, cross)
    real = mixed[:length, :half] - mixed[length:, half:]
    imag = mixed[length:, :half] + mixed[:length, half:]
    upper = jnp.concatenate([real.astype(jnp.bfloat16), imag.astype(jnp.bfloat16)], 1)
    surface = dot(upper, from_half_ref[...])
    weights = surface * surface
    out_ref[0, 0:1, :] = jnp.sum(weights, axis=0, keepdims=True)
    out_ref[0, 1:2, :] = jnp.sum(weights * offsets_ref[...], axis=0, keepdims=True)


def pair_flows(firsts, seconds, tables):
    count, length = firsts.shape[0], firsts.shape[-1]
    to_half, both, from_half = tables
    offsets = offsets_of(length)
    whole = lambda table: pl.BlockSpec(table.shape, lambda i: (0, 0))
    image = pl.BlockSpec((1, length, length), lambda i: (i, 0, 0))
    spread = jnp.broadcast_to(jnp.asarray(offsets)[:, None], (length, length))
    sums = pl.pallas_call(
        pair_kernel,
        grid=(count,),
        in_specs=[image, image, whole(to_half), whole(both), whole(from_half), whole(spread)],
        out_specs=pl.BlockSpec((1, 8, length), lambda i: (i, 0, 0)),
        out_shape=jax.ShapeDtypeStruct((count, 8, length), jnp.float32),
        compiler_params=pltpu.CompilerParams(vmem_limit_bytes=32 * 1024 * 1024),
        cost_estimate=pl.CostEstimate(
            flops=count * 18 * length**3, bytes_accessed=count * 4 * length**2, transcendentals=0
        ),
        name="pair_flows",
    )(firsts, seconds, to_half, both, from_half, spread)
    cells = float(length * length)
    total = jnp.sum(sums[:, 0], axis=1) / cells + epsilon
    along_rows = jnp.sum(sums[:, 1], axis=1) / cells / total
    along_cols = jnp.sum(sums[:, 0] * offsets, axis=1) / cells / total
    return jnp.stack([along_rows, along_cols], 0)


def exchange(x):
    return lax.all_to_all(x, "tile", split_axis=0, concat_axis=0, tiled=True)


def gathered(values):
    tiles = lax.axis_size("tile")
    return exchange(jnp.broadcast_to(values[None], (tiles,) + values.shape))


def per_device(strips, partner_tile, partner_strip, adjacency, start_positions):
    tiles = lax.axis_size("tile")
    tile_index = lax.axis_index("tile")
    own = strips[0]
    per_tile, length = own.shape[0], own.shape[1]
    half_strips = per_tile // 2
    tables = half_tables(length)
    partner = partner_tile[0] * per_tile + partner_strip[0]

    near_low = shifted(own[:half_strips], "sec", -1)
    back_high = shifted(own[half_strips:], "sec", 1)

    slices = own.reshape(per_tile, tiles, length // tiles, length).transpose(1, 0, 2, 3)
    spread = exchange(slices).reshape(tiles * per_tile, length // tiles, length)
    picked = jnp.take(spread, partner, axis=0).reshape(slices.shape)
    partners = exchange(picked).transpose(1, 0, 2, 3).reshape(own.shape)

    firsts = jnp.concatenate([near_low, own[half_strips:]], 0)
    seconds = jnp.concatenate([own[:half_strips], back_high], 0)
    depth_pairs = pair_flows(firsts, seconds, tables)
    depth_out = jnp.concatenate(
        [depth_pairs[:, :half_strips], shifted(depth_pairs[:, half_strips:], "sec", -1)], 1
    )
    plane_out = pair_flows(partners, own, tables)

    my_partner = lax.dynamic_slice_in_dim(partner, tile_index * per_tile, per_tile, 0)
    links = adjacency[:, 0, :]
    neighbours = links.shape[0]
    current = start_positions[:, 0, :]
    for iteration in range(STEPS):
        whole = gathered(current).transpose(1, 0, 2).reshape(2, tiles * per_tile)
        near_nodes = shifted(current, "sec", -1)
        springs = jnp.sum(whole[:, links], axis=1) - neighbours * current
        force = (
            springs
            + (whole[:, my_partner] + plane_out - current)
            + (near_nodes + depth_out - current)
        )
        current = current + relax_rate * force
    return (plane_out[:, None, :], depth_out[:, None, :], current[:, None, :])


def solution(mesh):
    return jax.shard_map(
        per_device,
        mesh=mesh,
        in_specs=(
            P("sec", "tile", None, None),
            P("sec", None),
            P("sec", None),
            P(None, "sec", "tile"),
            P(None, "sec", "tile"),
        ),
        out_specs=(P(None, "sec", "tile"), P(None, "sec", "tile"), P(None, "sec", "tile")),
        check_vma=False,
    )
```

```python
import functools
import math

import jax
import jax.numpy as jnp
import numpy as np
from jax import lax
from jax.experimental import pallas as pl
from jax.experimental.pallas import tpu as pltpu
from jax.sharding import PartitionSpec as P

STEPS = 2


epsilon = 1e-06
relax_rate = 0.1


def shifted(x, axis, by):
    devices = lax.axis_size(axis)
    return lax.ppermute(x, axis, [(i, (i + by) % devices) for i in range(devices)])


def offsets_of(length):
    return ((np.arange(length) + length // 2) % length - length // 2).astype(np.float32)


def angles_of(length):
    indices = np.arange(length)
    return (indices[:, None] * indices[None, :] % length) * (2.0 * math.pi / length)


def half_tables(length):
    half = length // 2
    cosine, sine = np.cos(angles_of(length)), np.sin(angles_of(length))
    to_half = np.concatenate([cosine[:, :half], -sine[:, :half]], 1)
    to_half[:, half] = cosine[:, half]
    from_half = np.concatenate([2.0 * cosine[:half], -2.0 * sine[:half]], 0)
    from_half[0] = 1.0
    from_half[half] = cosine[half]
    both = np.concatenate([cosine, sine], 0)
    return tuple(jnp.asarray(table, jnp.bfloat16) for table in (to_half, both, from_half))


def dot(left, right):
    return jnp.dot(left, right, preferred_element_type=jnp.float32)


def mixed_by(both, halves):
    length, half = both.shape[1], both.shape[1] // 2
    mixed = dot(both, halves)
    return (
        mixed[:length, :half],
        mixed[:length, half:],
        mixed[length:, :half],
        mixed[length:, half:],
    )


def fields_of(images, to_half, both):
    rows = [dot(image, to_half).astype(jnp.bfloat16) for image in images]
    parts = [mixed_by(both, row) for row in rows]
    fields = []
    for cos_re, cos_im, sin_re, sin_im in parts:
        first = lax.broadcasted_iota(jnp.int32, cos_re.shape, 1) == 0
        fields.append(
            tuple(
                field.astype(jnp.bfloat16)
                for field in (
                    jnp.where(first, cos_re, cos_re + sin_im),
                    jnp.where(first, sin_re, sin_re - cos_im),
                    jnp.where(first, cos_im, 0.0),
                    jnp.where(first, sin_im, 0.0),
                )
            )
        )
    return fields


def cross_of(a, b):
    a = [field.astype(jnp.float32) for field in a]
    b = [field.astype(jnp.float32) for field in b]
    real = a[0] * b[0] + a[1] * b[1] + a[2] * b[3] - a[3] * b[2]
    imag = a[1] * b[0] - a[0] * b[1] + a[2] * b[2] + a[3] * b[3]
    return jnp.concatenate([real.astype(jnp.bfloat16), imag.astype(jnp.bfloat16)], 1)


def store_sums(pairs, both, from_half, offsets, out_ref):
    crosses = [cross_of(first, second) for first, second in pairs]
    parts = [mixed_by(both, cross) for cross in crosses]
    uppers = [
        jnp.concatenate(
            [(cos_re - sin_im).astype(jnp.bfloat16), (sin_re + cos_im).astype(jnp.bfloat16)], 1
        )
        for cos_re, cos_im, sin_re, sin_im in parts
    ]
    for k, upper in enumerate(uppers):
        surface = dot(upper, from_half)
        weights = surface * surface
        out_ref[k, 0:1, :] = jnp.sum(weights, axis=0, keepdims=True)
        out_ref[k, 1:2, :] = jnp.sum(weights * offsets, axis=0, keepdims=True)


def split_fields(packed):
    half = packed.shape[-1] // 2
    return packed[0, :, :half], packed[0, :, half:], packed[1, :, :half], packed[1, :, half:]


def spectra_kernel(images_ref, to_half_ref, both_ref, out_ref):
    count = images_ref.shape[0]
    images = [images_ref[k] for k in range(count)]
    for k, (a, b, c, d) in enumerate(fields_of(images, to_half_ref[...], both_ref[...])):
        out_ref[k, 0] = jnp.concatenate([a, b], 1)
        out_ref[k, 1] = jnp.concatenate([c, d], 1)


def joined(pieces, k):
    rows = pieces.shape[0] // 2
    return jnp.concatenate(
        [
            jnp.concatenate([pieces[2 * r, k], pieces[2 * r + 1, k]], 1)
            for r in range(rows)
        ],
        0,
    )


def pair_kernel(
    other_first, in_pieces, images_ref, fields_ref, to_half_ref, both_ref, from_half_ref, offsets_ref, out_ref
):
    count = fields_ref.shape[0]
    if in_pieces:
        images = [joined(images_ref, k) for k in range(count)]
    else:
        images = [images_ref[k] for k in range(count)]
    others = fields_of(images, to_half_ref[...], both_ref[...])
    owns = [split_fields(fields_ref[k]) for k in range(count)]
    pairs = [(x, y) if other_first else (y, x) for x, y in zip(others, owns)]
    store_sums(pairs, both_ref[...], from_half_ref[...], offsets_ref[...], out_ref)


def whole(table):
    return pl.BlockSpec(table.shape, lambda i: (0,) * table.ndim)


def call_params():
    return pltpu.CompilerParams(vmem_limit_bytes=60 * 1024 * 1024)


def spectra_of(images, tables, batch=4):
    count, length = images.shape[0], images.shape[-1]
    to_half, both, _ = tables
    return pl.pallas_call(
        spectra_kernel,
        grid=(count // batch,),
        in_specs=[
            pl.BlockSpec((batch, length, length), lambda i: (i, 0, 0)),
            whole(to_half),
            whole(both),
        ],
        out_specs=pl.BlockSpec((batch, 2, length, length), lambda i: (i, 0, 0, 0)),
        out_shape=jax.ShapeDtypeStruct((count, 2, length, length), jnp.bfloat16),
        compiler_params=call_params(),
        cost_estimate=pl.CostEstimate(
            flops=count * 6 * length**3, bytes_accessed=count * 6 * length**2, transcendentals=0
        ),
        name="spectra",
    )(images, to_half, both)


def pair_sums(images, fields, start, other_first, tables, batch=4):
    in_pieces = images.ndim == 4
    count = images.shape[1] if in_pieces else images.shape[0]
    length = fields.shape[-1]
    to_half, both, from_half = tables
    spread = jnp.broadcast_to(jnp.asarray(offsets_of(length))[:, None], (length, length))
    if in_pieces:
        image_block = pl.BlockSpec(
            (images.shape[0], batch) + images.shape[2:], lambda i: (0, i, 0, 0)
        )
    else:
        image_block = pl.BlockSpec((batch, length, length), lambda i: (i, 0, 0))
    return pl.pallas_call(
        functools.partial(pair_kernel, other_first, in_pieces),
        grid=(count // batch,),
        in_specs=[
            image_block,
            pl.BlockSpec((batch, 2, length, length), lambda i: (i + start // batch, 0, 0, 0)),
            whole(to_half),
            whole(both),
            whole(from_half),
            whole(spread),
        ],
        out_specs=pl.BlockSpec((batch, 8, length), lambda i: (i, 0, 0)),
        out_shape=jax.ShapeDtypeStruct((count, 8, length), jnp.float32),
        compiler_params=call_params(),
        cost_estimate=pl.CostEstimate(
            flops=count * 12 * length**3, bytes_accessed=count * 6 * length**2, transcendentals=0
        ),
        name="pair_sums",
    )(images, fields, to_half, both, from_half, spread)


def flows_of(sums):
    length = sums.shape[-1]
    cells = float(length * length)
    total = jnp.sum(sums[:, 0], axis=1) / cells + epsilon
    along_rows = jnp.sum(sums[:, 1], axis=1) / cells / total
    along_cols = jnp.sum(sums[:, 0] * offsets_of(length), axis=1) / cells / total
    return jnp.stack([along_rows, along_cols], 0)


def cut_kernel(images_ref, note_ref, out_ref, held, read_sems, write_sem):
    pieces, slots, rows, columns = out_ref.shape
    count = slots - 1
    across = images_ref.shape[2] // columns
    chunks = read_sems.shape[0]
    batch = count // chunks

    def read(chunk):
        strips = pl.ds(chunk * batch, batch)
        return pltpu.make_async_copy(images_ref.at[strips], held.at[strips], read_sems.at[chunk])

    for chunk in range(chunks):
        read(chunk).start()
    writes = []
    for piece in range(pieces):
        write = pltpu.make_async_copy(
            note_ref, out_ref.at[piece, count], write_sem.at[len(writes)]
        )
        write.start()
        writes.append(write)
    for chunk in range(chunks):
        read(chunk).wait()
        strips = pl.ds(chunk * batch, batch)
        for piece in range(pieces):
            r, c = piece // across, piece % across
            write = pltpu.make_async_copy(
                held.at[strips, pl.ds(r * rows, rows), pl.ds(c * columns, columns)],
                out_ref.at[piece, strips],
                write_sem.at[len(writes)],
            )
            write.start()
            writes.append(write)
    for write in writes:
        write.wait()


def cut(images, note, pieces, chunks=4):
    count, length = images.shape[0], images.shape[-1]
    shape = (pieces, count + 1, 2 * length // pieces, length // 2)
    return pl.pallas_call(
        cut_kernel,
        in_specs=[
            pl.BlockSpec(memory_space=pl.ANY),
            pl.BlockSpec(memory_space=pltpu.VMEM),
        ],
        out_specs=pl.BlockSpec(memory_space=pl.ANY),
        out_shape=jax.ShapeDtypeStruct(shape, images.dtype),
        scratch_shapes=[
            pltpu.VMEM(images.shape, images.dtype),
            pltpu.SemaphoreType.DMA((chunks,)),
            pltpu.SemaphoreType.DMA(((chunks + 1) * pieces,)),
        ],
        compiler_params=pltpu.CompilerParams(vmem_limit_bytes=60 * 1024 * 1024),
        name="cut",
    )(images, note)


def exchange(x):
    return lax.all_to_all(x, "tile", split_axis=0, concat_axis=0, tiled=True)


def gathered(values):
    tiles = lax.axis_size("tile")
    spread = exchange(jnp.broadcast_to(values[None], (tiles,) + values.shape))
    return spread.transpose(1, 0, 2).reshape(values.shape[0], -1)


def in_parts(values, rows, columns):
    parts = []
    rest = values
    for _ in range(3):
        part = lax.reduce_precision(rest, 8, 7)
        parts.append(part.astype(jnp.bfloat16))
        rest = rest - part
    stacked = jnp.concatenate(parts, 0)
    return jnp.pad(stacked, ((0, rows - stacked.shape[0]), (0, columns - stacked.shape[1])))


def from_parts(tiles, height, width):
    parts = tiles[:, : 3 * height, :width].astype(jnp.float32)
    parts = parts.reshape(tiles.shape[0], 3, height, width)
    values = (parts[:, 2] + parts[:, 1]) + parts[:, 0]
    return values.transpose(1, 0, 2).reshape(height, -1)


def per_device(strips, partner_tile, partner_strip, adjacency, start_positions):
    tiles = lax.axis_size("tile")
    tile_index = lax.axis_index("tile")
    own = strips[0]
    per_tile, length = own.shape[0], own.shape[1]
    half_strips = per_tile // 2
    tables = half_tables(length)
    partner = partner_tile[0] * per_tile + partner_strip[0]
    my_partner = lax.dynamic_slice_in_dim(partner, tile_index * per_tile, per_tile, 0)
    links = adjacency[:, 0, :]
    neighbours = links.shape[0]
    start = start_positions[:, 0, :]

    def pull(whole_positions, current, near):
        springs = jnp.sum(whole_positions[:, links], axis=1) - neighbours * current
        return springs + (whole_positions[:, my_partner] - current) + (near - current)

    partner_rows = partner_tile[0] * (per_tile + 1) + partner_strip[0]

    near_low = shifted(own[:half_strips], "sec", -1)
    back_high = shifted(own[half_strips:], "sec", 1)

    rows, columns = 2 * length // tiles, length // 2
    pieces = cut(own, in_parts(start, rows, columns), tiles)
    spread = exchange(pieces)
    fields = spectra_of(own, tables)
    spread, fields, partner_rows = lax.optimization_barrier((spread, fields, partner_rows))
    picked = spread.reshape((-1, rows, columns)).at[partner_rows].get(mode="promise_in_bounds")
    partners = exchange(picked.reshape(tiles, per_tile, rows, columns))

    whole_start = from_parts(spread[:, per_tile], *start.shape)
    first_pull = pull(whole_start, start, shifted(start, "sec", -1))
    low = flows_of(pair_sums(near_low, fields, 0, True, tables))
    high = flows_of(pair_sums(back_high, fields, half_strips, False, tables))
    depth_out = jnp.concatenate([low, shifted(high, "sec", -1)], 1)
    partners, depth_out, first_pull = lax.optimization_barrier((partners, depth_out, first_pull))

    plane_out = flows_of(pair_sums(partners, fields, 0, True, tables))
    current = start + relax_rate * (first_pull + plane_out + depth_out)
    for iteration in range(1, STEPS):
        force = pull(gathered(current), current, shifted(current, "sec", -1))
        current = current + relax_rate * (force + plane_out + depth_out)
    return (plane_out[:, None, :], depth_out[:, None, :], current[:, None, :])


def solution(mesh):
    return jax.shard_map(
        per_device,
        mesh=mesh,
        in_specs=(
            P("sec", "tile", None, None),
            P("sec", None),
            P("sec", None),
            P(None, "sec", "tile"),
            P(None, "sec", "tile"),
        ),
        out_specs=(P(None, "sec", "tile"), P(None, "sec", "tile"), P(None, "sec", "tile")),
        check_vma=False,
    )
```

```python
import functools
import math

import jax
import jax.numpy as jnp
import numpy as np
from jax import lax
from jax.experimental import pallas as pl
from jax.experimental.pallas import tpu as pltpu
from jax.sharding import PartitionSpec as P

STEPS = 2


epsilon = 1e-06
relax_rate = 0.1


def shifted(x, axis, by):
    devices = lax.axis_size(axis)
    return lax.ppermute(x, axis, [(i, (i + by) % devices) for i in range(devices)])


def offsets_of(length):
    return ((np.arange(length) + length // 2) % length - length // 2).astype(np.float32)


def angles_of(length):
    indices = np.arange(length)
    return (indices[:, None] * indices[None, :] % length) * (2.0 * math.pi / length)


def half_tables(length):
    half = length // 2
    cosine, sine = np.cos(angles_of(length)), np.sin(angles_of(length))
    to_half = np.concatenate([cosine[:, :half], -sine[:, :half]], 1)
    to_half[:, half] = cosine[:, half]
    from_half = np.concatenate([2.0 * cosine[:half], -2.0 * sine[:half]], 0)
    from_half[0] = 1.0
    from_half[half] = cosine[half]
    both = np.concatenate([cosine, sine], 0)
    return tuple(jnp.asarray(table, jnp.bfloat16) for table in (to_half, both, from_half))


def dot(left, right):
    return jnp.dot(left, right, preferred_element_type=jnp.float32)


def mixed_by(both, halves):
    length, half = both.shape[1], both.shape[1] // 2
    mixed = dot(both, halves)
    return (
        mixed[:length, :half],
        mixed[:length, half:],
        mixed[length:, :half],
        mixed[length:, half:],
    )


def fields_of(images, to_half, both):
    rows = [dot(image, to_half).astype(jnp.bfloat16) for image in images]
    parts = [mixed_by(both, row) for row in rows]
    fields = []
    for cos_re, cos_im, sin_re, sin_im in parts:
        first = lax.broadcasted_iota(jnp.int32, cos_re.shape, 1) == 0
        fields.append(
            tuple(
                field.astype(jnp.bfloat16)
                for field in (
                    jnp.where(first, cos_re, cos_re + sin_im),
                    jnp.where(first, sin_re, sin_re - cos_im),
                    jnp.where(first, cos_im, 0.0),
                    jnp.where(first, sin_im, 0.0),
                )
            )
        )
    return fields


def cross_of(a, b):
    a = [field.astype(jnp.float32) for field in a]
    b = [field.astype(jnp.float32) for field in b]
    real = a[0] * b[0] + a[1] * b[1] + a[2] * b[3] - a[3] * b[2]
    imag = a[1] * b[0] - a[0] * b[1] + a[2] * b[2] + a[3] * b[3]
    return jnp.concatenate([real.astype(jnp.bfloat16), imag.astype(jnp.bfloat16)], 1)


def store_sums(pairs, both, from_half, offsets, out_ref):
    crosses = [cross_of(first, second) for first, second in pairs]
    parts = [mixed_by(both, cross) for cross in crosses]
    uppers = [
        jnp.concatenate(
            [(cos_re - sin_im).astype(jnp.bfloat16), (sin_re + cos_im).astype(jnp.bfloat16)], 1
        )
        for cos_re, cos_im, sin_re, sin_im in parts
    ]
    for k, upper in enumerate(uppers):
        surface = dot(upper, from_half)
        weights = surface * surface
        out_ref[k, 0:1, :] = jnp.sum(weights, axis=0, keepdims=True)
        out_ref[k, 1:2, :] = jnp.sum(weights * offsets, axis=0, keepdims=True)


def split_fields(packed):
    half = packed.shape[-1] // 2
    return packed[0, :, :half], packed[0, :, half:], packed[1, :, :half], packed[1, :, half:]


def spectra_kernel(images_ref, to_half_ref, both_ref, out_ref):
    count = images_ref.shape[0]
    images = [images_ref[k] for k in range(count)]
    for k, (a, b, c, d) in enumerate(fields_of(images, to_half_ref[...], both_ref[...])):
        out_ref[k, 0] = jnp.concatenate([a, b], 1)
        out_ref[k, 1] = jnp.concatenate([c, d], 1)


def pair_kernel(
    other_first, images_ref, fields_ref, to_half_ref, both_ref, from_half_ref, offsets_ref, out_ref
):
    count = fields_ref.shape[0]
    images = [images_ref[k] for k in range(count)]
    others = fields_of(images, to_half_ref[...], both_ref[...])
    owns = [split_fields(fields_ref[k]) for k in range(count)]
    pairs = [(x, y) if other_first else (y, x) for x, y in zip(others, owns)]
    store_sums(pairs, both_ref[...], from_half_ref[...], offsets_ref[...], out_ref)


def whole(table):
    return pl.BlockSpec(table.shape, lambda i: (0,) * table.ndim)


def call_params():
    return pltpu.CompilerParams(vmem_limit_bytes=60 * 1024 * 1024)


def spectra_of(images, tables, batch=4):
    count, length = images.shape[0], images.shape[-1]
    to_half, both, _ = tables
    return pl.pallas_call(
        spectra_kernel,
        grid=(count // batch,),
        in_specs=[
            pl.BlockSpec((batch, length, length), lambda i: (i, 0, 0)),
            whole(to_half),
            whole(both),
        ],
        out_specs=pl.BlockSpec((batch, 2, length, length), lambda i: (i, 0, 0, 0)),
        out_shape=jax.ShapeDtypeStruct((count, 2, length, length), jnp.bfloat16),
        compiler_params=call_params(),
        cost_estimate=pl.CostEstimate(
            flops=count * 6 * length**3, bytes_accessed=count * 6 * length**2, transcendentals=0
        ),
        name="spectra",
    )(images, to_half, both)


def pair_sums(images, fields, start, other_first, tables, batch=4):
    count, length = images.shape[0], images.shape[-1]
    to_half, both, from_half = tables
    spread = jnp.broadcast_to(jnp.asarray(offsets_of(length))[:, None], (length, length))
    return pl.pallas_call(
        functools.partial(pair_kernel, other_first),
        grid=(count // batch,),
        in_specs=[
            pl.BlockSpec((batch, length, length), lambda i: (i, 0, 0)),
            pl.BlockSpec((batch, 2, length, length), lambda i: (i + start // batch, 0, 0, 0)),
            whole(to_half),
            whole(both),
            whole(from_half),
            whole(spread),
        ],
        out_specs=pl.BlockSpec((batch, 8, length), lambda i: (i, 0, 0)),
        out_shape=jax.ShapeDtypeStruct((count, 8, length), jnp.float32),
        compiler_params=call_params(),
        cost_estimate=pl.CostEstimate(
            flops=count * 12 * length**3, bytes_accessed=count * 6 * length**2, transcendentals=0
        ),
        name="pair_sums",
    )(images, fields, to_half, both, from_half, spread)


def flows_of(sums):
    length = sums.shape[-1]
    cells = float(length * length)
    total = jnp.sum(sums[:, 0], axis=1) / cells + epsilon
    along_rows = jnp.sum(sums[:, 1], axis=1) / cells / total
    along_cols = jnp.sum(sums[:, 0] * offsets_of(length), axis=1) / cells / total
    return jnp.stack([along_rows, along_cols], 0)


def lines_kernel(images_ref, note_ref, table_ref, out_ref, held, lines, read_sems, write_sems):
    devices, slots, rows, _ = out_ref.shape
    count = slots - 1
    chunks = read_sems.shape[0]
    batch = count // chunks

    def read(chunk):
        strips = pl.ds(chunk * batch, batch)
        return pltpu.make_async_copy(images_ref.at[strips], held.at[strips], read_sems.at[chunk])

    for chunk in range(chunks):
        read(chunk).start()
    writes = []

    def write(source, target):
        copy = pltpu.make_async_copy(source, target, write_sems.at[len(writes)])
        copy.start()
        writes.append(copy)

    for device in range(devices):
        write(note_ref, out_ref.at[device, count])
    table = table_ref[...]
    for chunk in range(chunks):
        read(chunk).wait()
        for strip in range(chunk * batch, (chunk + 1) * batch):
            image = held[strip]
            across = lax.dot_general(
                table, image, (((1,), (1,)), ((), ())), preferred_element_type=jnp.float32
            )
            down = dot(table, image)
            for core, values in enumerate((across, down)):
                values = values.astype(jnp.bfloat16)
                for chip in range(devices // 2):
                    lines[2 * chip + core, strip] = values[chip * rows : (chip + 1) * rows]
        strips = pl.ds(chunk * batch, batch)
        for device in range(devices):
            write(lines.at[device, strips], out_ref.at[device, strips])
    for copy in writes:
        copy.wait()


def lines_of(images, note, table, devices, chunks=4):
    count, length = images.shape[0], images.shape[-1]
    rows = 2 * length // devices
    return pl.pallas_call(
        lines_kernel,
        in_specs=[
            pl.BlockSpec(memory_space=pl.ANY),
            pl.BlockSpec(memory_space=pltpu.VMEM),
            pl.BlockSpec(memory_space=pltpu.VMEM),
        ],
        out_specs=pl.BlockSpec(memory_space=pl.ANY),
        out_shape=jax.ShapeDtypeStruct((devices, count + 1, rows, length), jnp.bfloat16),
        scratch_shapes=[
            pltpu.VMEM(images.shape, images.dtype),
            pltpu.VMEM((devices, count, rows, length), jnp.bfloat16),
            pltpu.SemaphoreType.DMA((chunks,)),
            pltpu.SemaphoreType.DMA(((chunks + 1) * devices,)),
        ],
        compiler_params=call_params(),
        name="lines",
    )(images, note, table)


def moments_kernel(
    partner_ref, lines_ref, masks_ref, chosen_ref, both_ref, weights_ref, depth_ref, out_ref,
    held, spectra, extra, profile, read_sems,
):
    tiles, slots, rows, length = lines_ref.shape
    count = slots - 1
    half = rows // 2
    chunks = read_sems.shape[0]
    batch = tiles // chunks

    def read(chunk):
        part = pl.ds(chunk * batch, batch)
        return pltpu.make_async_copy(lines_ref.at[part], held.at[part], read_sems.at[chunk])

    for chunk in range(chunks):
        read(chunk).start()
    both = both_ref[...]
    plain, scale = masks_ref[0:half], masks_ref[half:rows]

    def transform(tile):
        mixed = dot(held[tile, :count].reshape(count * rows, length), both)
        mixed = mixed.reshape(count, rows, 2 * length)
        cos_re, sin_re = mixed[:, :half, :length], mixed[:, :half, length:]
        cos_im, sin_im = mixed[:, half:, :length], mixed[:, half:, length:]
        fields = jnp.concatenate([cos_re + sin_im * plain, sin_re - cos_im * plain], 1)
        at = pl.multiple_of(tile * count, count)
        spectra[pl.ds(at, count)] = fields.astype(jnp.bfloat16)
        extra[pl.ds(at, count), :] = mixed[:, half, :].astype(jnp.bfloat16)

    for chunk in range(chunks):
        read(chunk).wait()

        @pl.loop(0, batch // 2)
        def _(pair):
            transform(chunk * batch + 2 * pair)
            transform(chunk * batch + 2 * pair + 1)

    def surfaces(tile):
        at = pl.multiple_of(tile * count, count)
        first = jnp.stack([spectra[partner_ref[at + k]] for k in range(count)], 0)
        first = first.astype(jnp.float32)
        second = spectra[pl.ds(at, count)].astype(jnp.float32)
        a, b = first[:, :half], first[:, half:]
        c, d = second[:, :half], second[:, half:]
        cross = jnp.concatenate([a * c + b * d, b * c - a * d], 1).astype(jnp.bfloat16)
        mixed = dot(cross.reshape(count * rows, length), both).reshape(count, rows, 2 * length)
        real = mixed[:, :half, :length] - mixed[:, half:, length:]
        imag = mixed[:, :half, length:] + mixed[:, half:, :length]
        profile[pl.ds(at, count), :] = jnp.sum((real * real + imag * imag) * scale, axis=1)

    @pl.loop(0, tiles // 2)
    def _(pair):
        surfaces(2 * pair)
        surfaces(2 * pair + 1)

    second = extra[...]
    first = dot(chosen_ref[...], second)
    second = second.astype(jnp.float32)
    a, b = first[:, :length], first[:, length:]
    c, d = second[:, :length], second[:, length:]
    real = dot((a * c + b * d).astype(jnp.bfloat16), both[:, :length])
    imag = dot((b * c - a * d).astype(jnp.bfloat16), both[:, length:])
    last = real - imag
    profile[...] += last * last * masks_ref[rows : rows + 1]
    sums = lax.dot_general(
        weights_ref[...],
        profile[...],
        (((1,), (1,)), ((), ())),
        precision=lax.Precision.HIGHEST,
        preferred_element_type=jnp.float32,
    )
    sums = jnp.concatenate([sums[0:2], depth_ref[...]], 0)
    for tile in range(tiles):
        out_ref[tile] = sums


def moments_of(lines, partner, first_chip, depth, both, chunks=8):
    tiles, slots, rows, length = lines.shape
    count = slots - 1
    nodes = tiles * count
    half = rows // 2
    special = first_chip & (jnp.arange(half) == 0)
    masks = jnp.concatenate(
        [jnp.where(special, 0.0, 1.0), jnp.where(special, 1.0, 2.0), jnp.where(first_chip, 1.0, 0.0)[None]]
    )
    masks = jnp.broadcast_to(jnp.pad(masks, (0, half - 1))[:, None], (3 * half, length))
    chosen = (partner[:, None] == jnp.arange(nodes)).astype(jnp.bfloat16)
    weights = np.zeros((8, length), np.float32)
    weights[0] = 1.0
    weights[1] = offsets_of(length)
    vmem = pl.BlockSpec(memory_space=pltpu.VMEM)
    return pl.pallas_call(
        moments_kernel,
        in_specs=[
            pl.BlockSpec(memory_space=pltpu.SMEM),
            pl.BlockSpec(memory_space=pl.ANY),
            vmem,
            vmem,
            vmem,
            vmem,
            vmem,
        ],
        out_specs=vmem,
        out_shape=jax.ShapeDtypeStruct((tiles, 4, nodes), jnp.float32),
        scratch_shapes=[
            pltpu.VMEM(lines.shape, lines.dtype),
            pltpu.VMEM((nodes, rows, length), jnp.bfloat16),
            pltpu.VMEM((nodes, 2 * length), jnp.bfloat16),
            pltpu.VMEM((nodes, length), jnp.float32),
            pltpu.SemaphoreType.DMA((chunks,)),
        ],
        compiler_params=call_params(),
        cost_estimate=pl.CostEstimate(
            flops=nodes * rows * 4 * 2 * length**2, bytes_accessed=2 * lines.size, transcendentals=0
        ),
        name="moments",
    )(partner, lines, masks, chosen, both, jnp.asarray(weights), depth)


def pull_kernel(parts_ref, links_ref, own_ref, near_ref, out_ref):
    nodes = own_ref.shape[1]
    links = links_ref.shape[0]
    sources = lax.broadcasted_iota(jnp.int32, (nodes, nodes), 0)
    table = jnp.zeros((nodes, nodes), jnp.float32)
    for k in range(links):
        table += jnp.where(sources == links_ref[k : k + 1, :], 1.0, 0.0)
    sums = dot(parts_ref[...], table.astype(jnp.bfloat16))
    linked = (sums[4:6] + sums[2:4]) + sums[0:2]
    out_ref[...] = (linked - links * own_ref[...]) + (near_ref[...] - own_ref[...])


def pull_all(parts, links, own, near):
    return pl.pallas_call(
        pull_kernel,
        out_shape=jax.ShapeDtypeStruct(own.shape, jnp.float32),
        compiler_params=pltpu.CompilerParams(vmem_limit_bytes=32 * 1024 * 1024),
        name="pull",
    )(parts, links, own, near)


def exchange(x):
    return lax.all_to_all(x, "tile", split_axis=0, concat_axis=0, tiled=True)


def in_parts(values):
    parts = []
    rest = values
    for _ in range(3):
        part = lax.reduce_precision(rest, 8, 7)
        parts.append(part.astype(jnp.bfloat16))
        rest = rest - part
    return jnp.concatenate(parts, 0)


def note_of(start, links, rows, length):
    first = jnp.concatenate([in_parts(start), (links // 2).astype(jnp.bfloat16)], 0)
    second = (links % 2).astype(jnp.bfloat16)
    half = length // 2

    def padded(values):
        return jnp.pad(values, ((0, rows - values.shape[0]), (0, half - values.shape[1])))

    return jnp.concatenate([padded(first), padded(second)], 1)


def read_notes(notes, components, links, count):
    half = notes.shape[2] // 2
    first = notes[:, :, :count].transpose(1, 0, 2).reshape(notes.shape[1], -1)
    second = notes[:, :links, half : half + count].transpose(1, 0, 2).reshape(links, -1)
    height = 3 * components
    parts = first[:height]
    values = parts.astype(jnp.float32)
    start = (values[2 * components :] + values[components : 2 * components]) + values[:components]
    linked = 2 * first[height : height + links].astype(jnp.int32) + second.astype(jnp.int32)
    return parts, start, linked


def per_device(strips, partner_tile, partner_strip, adjacency, start_positions):
    tiles = lax.axis_size("tile")
    tile_index = lax.axis_index("tile")
    own = strips[0]
    per_tile, length = own.shape[0], own.shape[1]
    half_strips = per_tile // 2
    tables = half_tables(length)
    both = jnp.concatenate([tables[1][:length], tables[1][length:]], 1)
    partner = partner_tile[0] * per_tile + partner_strip[0]
    place = tile_index * per_tile
    links = adjacency[:, 0, :]
    start = start_positions[:, 0, :]

    rows = 2 * length // tiles
    order = np.arange(length).reshape(2, tiles // 2, rows // 2).transpose(1, 0, 2).reshape(-1)
    line_table = tables[0].T[order]
    lines = exchange(lines_of(own, note_of(start, links, rows, length), line_table, tiles))

    near_low = shifted(own[:half_strips], "sec", -1)
    back_high = shifted(own[half_strips:], "sec", 1)
    fields = spectra_of(own, tables)
    low = flows_of(pair_sums(near_low, fields, 0, True, tables))
    high = flows_of(pair_sums(back_high, fields, half_strips, False, tables))
    depth_out = jnp.concatenate([low, shifted(high, "sec", -1)], 1)
    depth_row = lax.dynamic_update_slice(
        jnp.zeros((2, tiles * per_tile), jnp.float32), depth_out, (0, place)
    )

    shares = moments_of(lines, partner, tile_index < 2, depth_row, both)
    parts, whole_start, whole_links = read_notes(
        lines[:, per_tile], start.shape[0], links.shape[0], per_tile
    )
    whole_links = jnp.concatenate([whole_links, partner[None]], 0)
    first_pull = pull_all(parts, whole_links, whole_start, shifted(whole_start, "sec", -1))

    received = exchange(shares).reshape(tiles // 2, 2, 4, tiles * per_tile)
    summed = jnp.sum(received, axis=0)
    plane_all = summed[:, 1] / length / (summed[:, 0] / length + epsilon)
    depth_all = summed[0, 2:] + summed[1, 2:]
    flow_all = plane_all + depth_all
    current = whole_start + relax_rate * (first_pull + flow_all)

    def mine(values):
        return lax.dynamic_slice_in_dim(values, place, per_tile, 1)

    my_links = jnp.concatenate([links, mine(partner[None])], 0)
    for iteration in range(1, STEPS):
        here = mine(current)
        linked = jnp.sum(current[:, my_links], axis=1)
        near = shifted(here, "sec", -1)
        force = (linked - my_links.shape[0] * here) + (near - here) + mine(flow_all)
        here = here + relax_rate * force
    return (mine(plane_all)[:, None, :], depth_out[:, None, :], here[:, None, :])


def solution(mesh):
    return jax.shard_map(
        per_device,
        mesh=mesh,
        in_specs=(
            P("sec", "tile", None, None),
            P("sec", None),
            P("sec", None),
            P(None, "sec", "tile"),
            P(None, "sec", "tile"),
        ),
        out_specs=(P(None, "sec", "tile"), P(None, "sec", "tile"), P(None, "sec", "tile")),
        check_vma=False,
    )
```

```python
import functools
import math

import jax
import jax.numpy as jnp
import numpy as np
from jax import lax
from jax.experimental import pallas as pl
from jax.experimental.pallas import tpu as pltpu
from jax.sharding import PartitionSpec as P

epsilon = 1e-06
relax_rate = 0.1


def shifted(x, axis, by):
    devices = lax.axis_size(axis)
    return lax.ppermute(x, axis, [(i, (i + by) % devices) for i in range(devices)])


def offsets_of(length):
    return ((np.arange(length) + length // 2) % length - length // 2).astype(np.float32)


def angles_of(length):
    indices = np.arange(length)
    return (indices[:, None] * indices[None, :] % length) * (2.0 * math.pi / length)


def half_tables(length):
    half = length // 2
    cosine, sine = np.cos(angles_of(length)), np.sin(angles_of(length))
    to_half = np.concatenate([cosine[:, :half], -sine[:, :half]], 1)
    to_half[:, half] = cosine[:, half]
    from_half = np.concatenate([2.0 * cosine[:half], -2.0 * sine[:half]], 0)
    from_half[0] = 1.0
    from_half[half] = cosine[half]
    both = np.concatenate([cosine, sine], 0)
    return tuple(jnp.asarray(table, jnp.bfloat16) for table in (to_half, both, from_half))


def dot(left, right):
    return jnp.dot(left, right, preferred_element_type=jnp.float32)


def mixed_by(both, halves):
    length, half = both.shape[1], both.shape[1] // 2
    mixed = dot(both, halves)
    return (
        mixed[:length, :half],
        mixed[:length, half:],
        mixed[length:, :half],
        mixed[length:, half:],
    )


def fields_of(images, to_half, both):
    rows = [dot(image, to_half).astype(jnp.bfloat16) for image in images]
    parts = [mixed_by(both, row) for row in rows]
    fields = []
    for cos_re, cos_im, sin_re, sin_im in parts:
        first = lax.broadcasted_iota(jnp.int32, cos_re.shape, 1) == 0
        fields.append(
            tuple(
                field.astype(jnp.bfloat16)
                for field in (
                    jnp.where(first, cos_re, cos_re + sin_im),
                    jnp.where(first, sin_re, sin_re - cos_im),
                    jnp.where(first, cos_im, 0.0),
                    jnp.where(first, sin_im, 0.0),
                )
            )
        )
    return fields


def cross_of(a, b):
    a = [field.astype(jnp.float32) for field in a]
    b = [field.astype(jnp.float32) for field in b]
    real = a[0] * b[0] + a[1] * b[1] + a[2] * b[3] - a[3] * b[2]
    imag = a[1] * b[0] - a[0] * b[1] + a[2] * b[2] + a[3] * b[3]
    return jnp.concatenate([real.astype(jnp.bfloat16), imag.astype(jnp.bfloat16)], 1)


def store_sums(pairs, both, from_half, offsets, out_ref):
    crosses = [cross_of(first, second) for first, second in pairs]
    parts = [mixed_by(both, cross) for cross in crosses]
    uppers = [
        jnp.concatenate(
            [(cos_re - sin_im).astype(jnp.bfloat16), (sin_re + cos_im).astype(jnp.bfloat16)], 1
        )
        for cos_re, cos_im, sin_re, sin_im in parts
    ]
    for k, upper in enumerate(uppers):
        surface = dot(upper, from_half)
        weights = surface * surface
        out_ref[k, 0:1, :] = jnp.sum(weights, axis=0, keepdims=True)
        out_ref[k, 1:2, :] = jnp.sum(weights * offsets, axis=0, keepdims=True)


def split_fields(packed):
    half = packed.shape[-1] // 2
    return packed[0, :, :half], packed[0, :, half:], packed[1, :, :half], packed[1, :, half:]


def spectra_kernel(images_ref, to_half_ref, both_ref, out_ref):
    count = images_ref.shape[0]
    images = [images_ref[k] for k in range(count)]
    for k, (a, b, c, d) in enumerate(fields_of(images, to_half_ref[...], both_ref[...])):
        out_ref[k, 0] = jnp.concatenate([a, b], 1)
        out_ref[k, 1] = jnp.concatenate([c, d], 1)


def pair_kernel(
    other_first, images_ref, fields_ref, to_half_ref, both_ref, from_half_ref, offsets_ref, out_ref
):
    count = fields_ref.shape[0]
    images = [images_ref[k] for k in range(count)]
    others = fields_of(images, to_half_ref[...], both_ref[...])
    owns = [split_fields(fields_ref[k]) for k in range(count)]
    pairs = [(x, y) if other_first else (y, x) for x, y in zip(others, owns)]
    store_sums(pairs, both_ref[...], from_half_ref[...], offsets_ref[...], out_ref)


def whole(table):
    return pl.BlockSpec(table.shape, lambda i: (0,) * table.ndim)


def call_params(megabytes=32):
    return pltpu.CompilerParams(vmem_limit_bytes=megabytes * 1024 * 1024)


def spectra_of(images, tables, batch=4):
    count, length = images.shape[0], images.shape[-1]
    to_half, both, _ = tables
    return pl.pallas_call(
        spectra_kernel,
        grid=(count // batch,),
        in_specs=[
            pl.BlockSpec((batch, length, length), lambda i: (i, 0, 0)),
            whole(to_half),
            whole(both),
        ],
        out_specs=pl.BlockSpec((batch, 2, length, length), lambda i: (i, 0, 0, 0)),
        out_shape=jax.ShapeDtypeStruct((count, 2, length, length), jnp.bfloat16),
        compiler_params=call_params(),
        cost_estimate=pl.CostEstimate(
            flops=count * 6 * length**3, bytes_accessed=count * 6 * length**2, transcendentals=0
        ),
        name="spectra",
    )(images, to_half, both)


def pair_sums(images, fields, start, other_first, tables, batch=4):
    count, length = images.shape[0], images.shape[-1]
    to_half, both, from_half = tables
    spread = jnp.broadcast_to(jnp.asarray(offsets_of(length))[:, None], (length, length))
    return pl.pallas_call(
        functools.partial(pair_kernel, other_first),
        grid=(count // batch,),
        in_specs=[
            pl.BlockSpec((batch, length, length), lambda i: (i, 0, 0)),
            pl.BlockSpec((batch, 2, length, length), lambda i: (i + start // batch, 0, 0, 0)),
            whole(to_half),
            whole(both),
            whole(from_half),
            whole(spread),
        ],
        out_specs=pl.BlockSpec((batch, 8, length), lambda i: (i, 0, 0)),
        out_shape=jax.ShapeDtypeStruct((count, 8, length), jnp.float32),
        compiler_params=call_params(),
        cost_estimate=pl.CostEstimate(
            flops=count * 12 * length**3, bytes_accessed=count * 6 * length**2, transcendentals=0
        ),
        name="pair_sums",
    )(images, fields, to_half, both, from_half, spread)


def flows_of(sums):
    length = sums.shape[-1]
    cells = float(length * length)
    total = jnp.sum(sums[:, 0], axis=1) / cells + epsilon
    along_rows = jnp.sum(sums[:, 1], axis=1) / cells / total
    along_cols = jnp.sum(sums[:, 0] * offsets_of(length), axis=1) / cells / total
    return jnp.stack([along_rows, along_cols], 0)


def lines_kernel(
    images_ref, start_ref, table_ref, out_ref, held, lines, note, read_sems, write_sems
):
    devices, slots, rows, columns = out_ref.shape
    count = slots // 2
    chunks = read_sems.shape[0]
    batch = count // chunks

    def read(chunk):
        strips = pl.ds(chunk * batch, batch)
        return pltpu.make_async_copy(images_ref.at[strips], held.at[strips], read_sems.at[chunk])

    for chunk in range(chunks):
        read(chunk).start()

    height, nodes = start_ref.shape
    note[...] = jnp.zeros_like(note)
    rest = start_ref[...]
    for part in range(3):
        rounded = rest.astype(jnp.bfloat16).astype(jnp.float32)
        note[part * height : (part + 1) * height, :nodes] = rounded
        rest = rest - rounded
    packed = note[...].astype(jnp.bfloat16)
    for device in range(devices):
        lines[device, 2 * count] = packed

    writes = []

    def write(first, number):
        part = pl.ds(first, number)
        copy = pltpu.make_async_copy(
            lines.at[:, part], out_ref.at[:, part], write_sems.at[len(writes)]
        )
        copy.start()
        writes.append(copy)

    write(2 * count, 1)
    table = table_ref[...]
    for chunk in range(chunks):
        read(chunk).wait()
        for strip in range(chunk * batch, (chunk + 1) * batch):
            image = held[strip]
            across = lax.dot_general(
                table, image, (((1,), (1,)), ((), ())), preferred_element_type=jnp.float32
            )
            down = dot(table, image)
            for core, values in enumerate((across, down)):
                values = values.astype(jnp.bfloat16)
                for chip in range(devices // 2):
                    piece = values[chip * rows : (chip + 1) * rows]
                    lines[2 * chip + core, strip] = piece[:, :columns]
                    lines[2 * chip + core, count + strip] = piece[:, columns:]
        write(chunk * batch, batch)
        write(count + chunk * batch, batch)
    for copy in writes:
        copy.wait()


def lines_of(images, start, table, devices, chunks=4):
    count, length = images.shape[0], images.shape[-1]
    rows = 2 * length // devices
    shape = (devices, 2 * count + 1, rows, length // 2)
    vmem = pl.BlockSpec(memory_space=pltpu.VMEM)
    return pl.pallas_call(
        lines_kernel,
        in_specs=[pl.BlockSpec(memory_space=pl.ANY), vmem, vmem],
        out_specs=pl.BlockSpec(memory_space=pl.ANY),
        out_shape=jax.ShapeDtypeStruct(shape, jnp.bfloat16),
        scratch_shapes=[
            pltpu.VMEM(images.shape, images.dtype),
            pltpu.VMEM(shape, jnp.bfloat16),
            pltpu.VMEM((rows, length // 2), jnp.float32),
            pltpu.SemaphoreType.DMA((chunks,)),
            pltpu.SemaphoreType.DMA((2 * chunks + 1,)),
        ],
        compiler_params=call_params(60),
        cost_estimate=pl.CostEstimate(
            flops=count * 4 * length**3, bytes_accessed=count * 6 * length**2, transcendentals=0
        ),
        name="lines",
    )(images, start, table)


def moments_kernel(
    partner_ref, place_ref, lines_ref, chosen_ref, both_ref, weights_ref, counts_ref, rest_ref, out_ref,
    spectra, extra, profile,
):
    tiles, slots, rows, columns = lines_ref.shape
    count, length = slots // 2, 2 * columns
    half = rows // 2
    unroll = math.gcd(tiles, 8)
    both = both_ref[...]
    place = place_ref[0]
    on_first = (place < 2 * count).astype(jnp.int32)
    special = (lax.broadcasted_iota(jnp.int32, (half, length), 0) == 0) & (on_first == 1)
    plain = jnp.where(special, 0.0, 1.0)
    scale = jnp.where(special, 1.0, 2.0)

    def transform(tile):
        lines = jnp.concatenate(
            [lines_ref[tile, :count], lines_ref[tile, count : 2 * count]], 2
        )
        mixed = dot(lines.reshape(count * rows, length), both)
        mixed = mixed.reshape(count, rows, 2 * length)
        cos_re, sin_re = mixed[:, :half, :length], mixed[:, :half, length:]
        cos_im, sin_im = mixed[:, half:, :length], mixed[:, half:, length:]
        fields = jnp.concatenate([cos_re + sin_im * plain, sin_re - cos_im * plain], 1)
        at = pl.multiple_of(tile * count, count)
        spectra[pl.ds(at, count)] = fields.astype(jnp.bfloat16)
        extra[pl.ds(at, count), :] = mixed[:, half, :].astype(jnp.bfloat16)

    @pl.loop(0, tiles // unroll)
    def _(step):
        for k in range(unroll):
            transform(step * unroll + k)

    def surfaces(tile):
        at = pl.multiple_of(tile * count, count)
        first = jnp.stack([spectra[partner_ref[at + k]] for k in range(count)], 0)
        first = first.astype(jnp.float32)
        second = spectra[pl.ds(at, count)].astype(jnp.float32)
        a, b = first[:, :half], first[:, half:]
        c, d = second[:, :half], second[:, half:]
        cross = jnp.concatenate([a * c + b * d, b * c - a * d], 1).astype(jnp.bfloat16)
        mixed = dot(cross.reshape(count * rows, length), both).reshape(count, rows, 2 * length)
        real = mixed[:, :half, :length] - mixed[:, half:, length:]
        imag = mixed[:, :half, length:] + mixed[:, half:, :length]
        profile[pl.ds(at, count), :] = jnp.sum((real * real + imag * imag) * scale, axis=1)

    @pl.loop(0, tiles // unroll)
    def _(step):
        for k in range(unroll):
            surfaces(step * unroll + k)

    second = extra[...]
    first = dot(chosen_ref[...], second)
    second = second.astype(jnp.float32)
    a, b = first[:, :length], first[:, length:]
    c, d = second[:, :length], second[:, length:]
    real = dot((a * c + b * d).astype(jnp.bfloat16), both[:, :length])
    imag = dot((b * c - a * d).astype(jnp.bfloat16), both[:, length:])
    last = real - imag
    profile[...] += last * last * on_first.astype(jnp.float32)
    sums = lax.dot_general(
        weights_ref[...],
        profile[...],
        (((1,), (1,)), ((), ())),
        precision=lax.Precision.HIGHEST,
        preferred_element_type=jnp.float32,
    )
    linked = jnp.zeros((rows, columns), jnp.float32)
    for tile in range(tiles):
        linked += dot(lines_ref[tile, 2 * count], counts_ref[tile])
    linked = (linked[4:6] + linked[2:4]) + linked[0:2]
    base = jnp.concatenate([rest_ref[0:2] + relax_rate * linked, rest_ref[2:8]], 0)
    base = jnp.concatenate([base, jnp.zeros((8, tiles * count - columns), jnp.float32)], 1)
    base = pltpu.roll(base, place, 1)
    sums = jnp.concatenate([sums[0:2], base[0:2]], 0)
    for tile in range(tiles):
        out_ref[tile] = sums


def moments_of(lines, partner, place, links, rest, both):
    tiles, slots, rows, columns = lines.shape
    count, length = slots // 2, 2 * columns
    nodes = tiles * count
    chosen = (partner[:, None] == jnp.arange(nodes)).astype(jnp.bfloat16)
    weights = np.zeros((8, length), np.float32)
    weights[0] = 1.0
    weights[1] = offsets_of(length)
    lanes = np.arange(columns)
    sources = jnp.asarray(np.where(lanes < count, np.arange(tiles)[:, None] * count + lanes, -1))
    links = jnp.pad(links, ((0, 0), (0, columns - count)), constant_values=nodes)
    counts = sum(sources[:, :, None] == links[k] for k in range(links.shape[0])).astype(jnp.bfloat16)
    rest = jnp.pad(rest, ((0, 8 - rest.shape[0]), (0, columns - count)))
    vmem = pl.BlockSpec(memory_space=pltpu.VMEM)
    smem = pl.BlockSpec(memory_space=pltpu.SMEM)
    return pl.pallas_call(
        moments_kernel,
        in_specs=[smem, smem, vmem, vmem, vmem, vmem, vmem, vmem],
        out_specs=vmem,
        out_shape=jax.ShapeDtypeStruct((tiles, 4, nodes), jnp.float32),
        scratch_shapes=[
            pltpu.VMEM((nodes, rows, length), jnp.bfloat16),
            pltpu.VMEM((nodes, 2 * length), jnp.bfloat16),
            pltpu.VMEM((nodes, length), jnp.float32),
        ],
        compiler_params=call_params(),
        cost_estimate=pl.CostEstimate(
            flops=nodes * rows * 4 * 2 * length**2, bytes_accessed=2 * lines.size, transcendentals=0
        ),
        name="moments",
    )(partner, place[None], lines, chosen, both, jnp.asarray(weights), counts, rest)


def exchange(x):
    return lax.all_to_all(x, "tile", split_axis=0, concat_axis=0, tiled=True)


def per_device(strips, partner_tile, partner_strip, adjacency, start_positions):
    tiles = lax.axis_size("tile")
    tile_index = lax.axis_index("tile")
    own = strips[0]
    per_tile, length = own.shape[0], own.shape[1]
    half_strips = per_tile // 2
    tables = half_tables(length)
    both = jnp.concatenate([tables[1][:length], tables[1][length:]], 1)
    partner = partner_tile[0] * per_tile + partner_strip[0]
    place = tile_index * per_tile
    links = adjacency[:, 0, :]
    start = start_positions[:, 0, :]

    rows = 2 * length // tiles
    order = np.arange(length).reshape(2, tiles // 2, rows // 2).transpose(1, 0, 2).reshape(-1)
    line_table = tables[0].T[order]
    lines = exchange(lines_of(own, start, line_table, tiles))

    near_low = shifted(own[:half_strips], "sec", -1)
    back_high = shifted(own[half_strips:], "sec", 1)
    strips_here, near_low, back_high = lax.optimization_barrier((own, near_low, back_high))
    fields = spectra_of(strips_here, tables)
    low = flows_of(pair_sums(near_low, fields, 0, True, tables))
    high = flows_of(pair_sums(back_high, fields, half_strips, False, tables))
    depth_out = jnp.concatenate([low, shifted(high, "sec", -1)], 1)

    def mine(values):
        return lax.dynamic_slice_in_dim(values, place, per_tile, 1)

    links = jnp.concatenate([links, mine(partner[None])], 0)
    number = links.shape[0]
    near = shifted(start, "sec", -1)
    rest = start + relax_rate * ((near - start) - number * start + depth_out)

    shares = exchange(moments_of(lines, partner, place, links, rest, both))
    summed = jnp.sum(shares.reshape(tiles // 2, 2, 4, tiles * per_tile), axis=0)
    plane_all = summed[:, 1] / length / (summed[:, 0] / length + epsilon)
    current = summed[0, 2:] + summed[1, 2:] + relax_rate * plane_all

    plane_out, here = mine(plane_all), mine(current)
    linked = jnp.sum(current[:, links], axis=1)
    near = shifted(here, "sec", -1)
    here = here + relax_rate * (
        (linked - number * here) + (near - here) + plane_out + depth_out
    )
    return (plane_out[:, None, :], depth_out[:, None, :], here[:, None, :])


def solution(mesh):
    return jax.shard_map(
        per_device,
        mesh=mesh,
        in_specs=(
            P("sec", "tile", None, None),
            P("sec", None),
            P("sec", None),
            P(None, "sec", "tile"),
            P(None, "sec", "tile"),
        ),
        out_specs=(P(None, "sec", "tile"), P(None, "sec", "tile"), P(None, "sec", "tile")),
        check_vma=False,
    )
```

```python
import functools
import math

import jax
import jax.numpy as jnp
import numpy as np
from jax import lax
from jax.experimental import pallas as pl
from jax.experimental.pallas import tpu as pltpu
from jax.sharding import PartitionSpec as P

epsilon = 1e-06
relax_rate = 0.1


def shifted(x, axis, by):
    devices = lax.axis_size(axis)
    return lax.ppermute(x, axis, [(i, (i + by) % devices) for i in range(devices)])


def offsets_of(length):
    return ((np.arange(length) + length // 2) % length - length // 2).astype(np.float32)


def angles_of(length):
    indices = np.arange(length)
    return (indices[:, None] * indices[None, :] % length) * (2.0 * math.pi / length)


def half_tables(length):
    half = length // 2
    cosine, sine = np.cos(angles_of(length)), np.sin(angles_of(length))
    to_half = np.concatenate([cosine[:, :half], -sine[:, :half]], 1)
    to_half[:, half] = cosine[:, half]
    from_half = np.concatenate([2.0 * cosine[:half], -2.0 * sine[:half]], 0)
    from_half[0] = 1.0
    from_half[half] = cosine[half]
    both = np.concatenate([cosine, sine], 0)
    return tuple(jnp.asarray(table, jnp.bfloat16) for table in (to_half, both, from_half))


def dot(left, right):
    return jnp.dot(left, right, preferred_element_type=jnp.float32)


def mixed_by(both, halves):
    length, half = both.shape[1], both.shape[1] // 2
    mixed = dot(both, halves)
    return (
        mixed[:length, :half],
        mixed[:length, half:],
        mixed[length:, :half],
        mixed[length:, half:],
    )


def fields_of(images, to_half, both):
    rows = [dot(image, to_half).astype(jnp.bfloat16) for image in images]
    parts = [mixed_by(both, row) for row in rows]
    fields = []
    for cos_re, cos_im, sin_re, sin_im in parts:
        first = lax.broadcasted_iota(jnp.int32, cos_re.shape, 1) == 0
        fields.append(
            tuple(
                field.astype(jnp.bfloat16)
                for field in (
                    jnp.where(first, cos_re, cos_re + sin_im),
                    jnp.where(first, sin_re, sin_re - cos_im),
                    jnp.where(first, cos_im, 0.0),
                    jnp.where(first, sin_im, 0.0),
                )
            )
        )
    return fields


def cross_of(a, b):
    a = [field.astype(jnp.float32) for field in a]
    b = [field.astype(jnp.float32) for field in b]
    real = a[0] * b[0] + a[1] * b[1] + a[2] * b[3] - a[3] * b[2]
    imag = a[1] * b[0] - a[0] * b[1] + a[2] * b[2] + a[3] * b[3]
    return jnp.concatenate([real.astype(jnp.bfloat16), imag.astype(jnp.bfloat16)], 1)


def store_sums(pairs, both, from_half, offsets, out_ref):
    crosses = [cross_of(first, second) for first, second in pairs]
    parts = [mixed_by(both, cross) for cross in crosses]
    uppers = [
        jnp.concatenate(
            [(cos_re - sin_im).astype(jnp.bfloat16), (sin_re + cos_im).astype(jnp.bfloat16)], 1
        )
        for cos_re, cos_im, sin_re, sin_im in parts
    ]
    for k, upper in enumerate(uppers):
        surface = dot(upper, from_half)
        weights = surface * surface
        out_ref[k, 0:1, :] = jnp.sum(weights, axis=0, keepdims=True)
        out_ref[k, 1:2, :] = jnp.sum(weights * offsets, axis=0, keepdims=True)


def split_fields(packed):
    half = packed.shape[-1] // 2
    return packed[0, :, :half], packed[0, :, half:], packed[1, :, :half], packed[1, :, half:]


def spectra_kernel(images_ref, to_half_ref, both_ref, out_ref):
    count = images_ref.shape[0]
    images = [images_ref[k] for k in range(count)]
    for k, (a, b, c, d) in enumerate(fields_of(images, to_half_ref[...], both_ref[...])):
        out_ref[k, 0] = jnp.concatenate([a, b], 1)
        out_ref[k, 1] = jnp.concatenate([c, d], 1)


def pair_kernel(
    other_first, images_ref, fields_ref, to_half_ref, both_ref, from_half_ref, offsets_ref, out_ref
):
    count = fields_ref.shape[0]
    images = [images_ref[k] for k in range(count)]
    others = fields_of(images, to_half_ref[...], both_ref[...])
    owns = [split_fields(fields_ref[k]) for k in range(count)]
    pairs = [(x, y) if other_first else (y, x) for x, y in zip(others, owns)]
    store_sums(pairs, both_ref[...], from_half_ref[...], offsets_ref[...], out_ref)


def whole(table):
    return pl.BlockSpec(table.shape, lambda i: (0,) * table.ndim)


def call_params(megabytes=32):
    return pltpu.CompilerParams(vmem_limit_bytes=megabytes * 1024 * 1024)


def spectra_of(images, tables, batch=4):
    count, length = images.shape[0], images.shape[-1]
    to_half, both, _ = tables
    return pl.pallas_call(
        spectra_kernel,
        grid=(count // batch,),
        in_specs=[
            pl.BlockSpec((batch, length, length), lambda i: (i, 0, 0)),
            whole(to_half),
            whole(both),
        ],
        out_specs=pl.BlockSpec((batch, 2, length, length), lambda i: (i, 0, 0, 0)),
        out_shape=jax.ShapeDtypeStruct((count, 2, length, length), jnp.bfloat16),
        compiler_params=call_params(),
        cost_estimate=pl.CostEstimate(
            flops=count * 6 * length**3, bytes_accessed=count * 6 * length**2, transcendentals=0
        ),
        name="spectra",
    )(images, to_half, both)


def pair_sums(images, fields, start, other_first, tables, batch=4):
    count, length = images.shape[0], images.shape[-1]
    to_half, both, from_half = tables
    spread = jnp.broadcast_to(jnp.asarray(offsets_of(length))[:, None], (length, length))
    return pl.pallas_call(
        functools.partial(pair_kernel, other_first),
        grid=(count // batch,),
        in_specs=[
            pl.BlockSpec((batch, length, length), lambda i: (i, 0, 0)),
            pl.BlockSpec((batch, 2, length, length), lambda i: (i + start // batch, 0, 0, 0)),
            whole(to_half),
            whole(both),
            whole(from_half),
            whole(spread),
        ],
        out_specs=pl.BlockSpec((batch, 8, length), lambda i: (i, 0, 0)),
        out_shape=jax.ShapeDtypeStruct((count, 8, length), jnp.float32),
        compiler_params=call_params(),
        cost_estimate=pl.CostEstimate(
            flops=count * 12 * length**3, bytes_accessed=count * 6 * length**2, transcendentals=0
        ),
        name="pair_sums",
    )(images, fields, to_half, both, from_half, spread)


def flows_of(sums):
    length = sums.shape[-1]
    cells = float(length * length)
    total = jnp.sum(sums[:, 0], axis=1) / cells + epsilon
    along_rows = jnp.sum(sums[:, 1], axis=1) / cells / total
    along_cols = jnp.sum(sums[:, 0] * offsets_of(length), axis=1) / cells / total
    return jnp.stack([along_rows, along_cols], 0)


def lines_kernel(
    images_ref, start_ref, table_ref, out_ref, held, lines, note, read_sems, write_sems
):
    devices, slots, rows, columns = out_ref.shape
    count = slots // 2
    chunks = read_sems.shape[0]
    batch = count // chunks

    def read(chunk):
        strips = pl.ds(chunk * batch, batch)
        return pltpu.make_async_copy(images_ref.at[strips], held.at[strips], read_sems.at[chunk])

    for chunk in range(chunks):
        read(chunk).start()

    height, nodes = start_ref.shape
    note[...] = jnp.zeros_like(note)
    rest = start_ref[...]
    for part in range(3):
        rounded = rest.astype(jnp.bfloat16).astype(jnp.float32)
        note[part * height : (part + 1) * height, :nodes] = rounded
        rest = rest - rounded
    packed = note[...].astype(jnp.bfloat16)
    for device in range(devices):
        lines[device, 2 * count] = packed

    writes = []

    def write(first, number):
        part = pl.ds(first, number)
        copy = pltpu.make_async_copy(
            lines.at[:, part], out_ref.at[:, part], write_sems.at[len(writes)]
        )
        copy.start()
        writes.append(copy)

    write(2 * count, 1)
    table = table_ref[...]
    for chunk in range(chunks):
        read(chunk).wait()
        for strip in range(chunk * batch, (chunk + 1) * batch):
            image = held[strip]
            across = lax.dot_general(
                table, image, (((1,), (1,)), ((), ())), preferred_element_type=jnp.float32
            )
            down = dot(table, image)
            for core, values in enumerate((across, down)):
                values = values.astype(jnp.bfloat16)
                for chip in range(devices // 2):
                    piece = values[chip * rows : (chip + 1) * rows]
                    lines[2 * chip + core, strip] = piece[:, :columns]
                    lines[2 * chip + core, count + strip] = piece[:, columns:]
        write(chunk * batch, batch)
        write(count + chunk * batch, batch)
    for copy in writes:
        copy.wait()


def lines_of(images, start, table, devices, chunks=4):
    count, length = images.shape[0], images.shape[-1]
    rows = 2 * length // devices
    shape = (devices, 2 * count + 1, rows, length // 2)
    vmem = pl.BlockSpec(memory_space=pltpu.VMEM)
    return pl.pallas_call(
        lines_kernel,
        in_specs=[pl.BlockSpec(memory_space=pl.ANY), vmem, vmem],
        out_specs=pl.BlockSpec(memory_space=pl.ANY),
        out_shape=jax.ShapeDtypeStruct(shape, jnp.bfloat16),
        scratch_shapes=[
            pltpu.VMEM(images.shape, images.dtype),
            pltpu.VMEM(shape, jnp.bfloat16),
            pltpu.VMEM((rows, length // 2), jnp.float32),
            pltpu.SemaphoreType.DMA((chunks,)),
            pltpu.SemaphoreType.DMA((2 * chunks + 1,)),
        ],
        compiler_params=call_params(60),
        cost_estimate=pl.CostEstimate(
            flops=count * 4 * length**3, bytes_accessed=count * 6 * length**2, transcendentals=0
        ),
        name="lines",
    )(images, start, table)


def moments_kernel(
    partner_ref, place_ref, lines_ref, chosen_ref, both_ref, weights_ref, counts_ref, rest_ref, out_ref,
    spectra, extra, profile,
):
    tiles, slots, rows, columns = lines_ref.shape
    count, length = slots // 2, 2 * columns
    half = rows // 2
    unroll = math.gcd(tiles, 16)
    both = both_ref[...]
    place = place_ref[0]
    on_first = (place < 2 * count).astype(jnp.int32)
    special = (lax.broadcasted_iota(jnp.int32, (half, length), 0) == 0) & (on_first == 1)
    plain = jnp.where(special, 0.0, 1.0)
    scale = jnp.where(special, 1.0, 2.0)

    def transform(tile):
        lines = jnp.concatenate(
            [lines_ref[tile, :count], lines_ref[tile, count : 2 * count]], 2
        )
        mixed = dot(lines.reshape(count * rows, length), both)
        mixed = mixed.reshape(count, rows, 2 * length)
        cos_re, sin_re = mixed[:, :half, :length], mixed[:, :half, length:]
        cos_im, sin_im = mixed[:, half:, :length], mixed[:, half:, length:]
        fields = jnp.concatenate([cos_re + sin_im * plain, sin_re - cos_im * plain], 1)
        at = pl.multiple_of(tile * count, count)
        spectra[pl.ds(at, count)] = fields.astype(jnp.bfloat16)
        extra[pl.ds(at, count), :] = mixed[:, half, :].astype(jnp.bfloat16)

    @pl.loop(0, tiles // unroll)
    def _(step):
        for k in range(unroll):
            transform(step * unroll + k)

    def surfaces(tile):
        at = pl.multiple_of(tile * count, count)
        first = jnp.stack([spectra[partner_ref[at + k]] for k in range(count)], 0)
        first = first.astype(jnp.float32)
        second = spectra[pl.ds(at, count)].astype(jnp.float32)
        a, b = first[:, :half], first[:, half:]
        c, d = second[:, :half], second[:, half:]
        cross = jnp.concatenate([a * c + b * d, b * c - a * d], 1).astype(jnp.bfloat16)
        mixed = dot(cross.reshape(count * rows, length), both).reshape(count, rows, 2 * length)
        real = mixed[:, :half, :length] - mixed[:, half:, length:]
        imag = mixed[:, :half, length:] + mixed[:, half:, :length]
        profile[pl.ds(at, count), :] = jnp.sum((real * real + imag * imag) * scale, axis=1)

    @pl.loop(0, tiles // unroll)
    def _(step):
        for k in range(unroll):
            surfaces(step * unroll + k)

    second = extra[...]
    first = dot(chosen_ref[...], second)
    second = second.astype(jnp.float32)
    a, b = first[:, :length], first[:, length:]
    c, d = second[:, :length], second[:, length:]
    real = dot((a * c + b * d).astype(jnp.bfloat16), both[:, :length])
    imag = dot((b * c - a * d).astype(jnp.bfloat16), both[:, length:])
    last = real - imag
    profile[...] += last * last * on_first.astype(jnp.float32)
    sums = lax.dot_general(
        weights_ref[...],
        profile[...],
        (((1,), (1,)), ((), ())),
        precision=lax.Precision.HIGHEST,
        preferred_element_type=jnp.float32,
    )
    linked = jnp.zeros((rows, columns), jnp.float32)
    for tile in range(tiles):
        linked += dot(lines_ref[tile, 2 * count], counts_ref[tile])
    linked = (linked[4:6] + linked[2:4]) + linked[0:2]
    base = rest_ref[...] + relax_rate * linked
    width = count
    while width < columns:
        base += pltpu.roll(base, width, 1)
        width *= 2

    def folded(row):
        return jnp.concatenate(
            [sums[row : row + 1, at : at + columns] for at in range(0, tiles * count, columns)], 0
        )

    packed = jnp.concatenate([folded(0), *two_parts(folded(1)), *two_parts(base)], 0)
    packed = packed.astype(jnp.bfloat16)
    for tile in range(tiles):
        out_ref[tile] = packed


def two_parts(values):
    high = values.astype(jnp.bfloat16).astype(jnp.float32)
    return high, values - high


def finish_kernel(shares_ref, out_ref):
    tiles, _, columns = shares_ref.shape
    nodes = out_ref.shape[1]
    folds = nodes // columns
    count = nodes // tiles
    length = 2 * columns
    shares = [shares_ref[tile].astype(jnp.float32) for tile in range(tiles)]
    owner = lax.broadcasted_iota(jnp.int32, (2, columns), 1) // count
    flows = []
    for core in range(2):
        total = sum(shares[core + 2 :: 2], shares[core])
        moment = total[folds : 2 * folds] + total[2 * folds : 3 * folds]
        flows.append(moment / length / (total[:folds] / length + epsilon))
    first = 3 * folds
    for fold in range(folds):
        at = pl.ds(fold * columns, columns)
        base = jnp.zeros((2, columns), jnp.float32)
        for k in range(columns // count):
            share = shares[fold * (columns // count) + k]
            position = share[first : first + 2] + share[first + 2 : first + 4]
            base += jnp.where(owner == k, position, 0.0)
        flow = jnp.concatenate([part[fold : fold + 1] for part in flows], 0)
        out_ref[0:2, at] = flow
        out_ref[2:4, at] = base + relax_rate * flow


def finish(shares, nodes):
    return pl.pallas_call(
        finish_kernel,
        out_shape=jax.ShapeDtypeStruct((4, nodes), jnp.float32),
        compiler_params=call_params(),
        name="finish",
    )(shares)


def moments_of(lines, partner, place, links, rest, both):
    tiles, slots, rows, columns = lines.shape
    count, length = slots // 2, 2 * columns
    nodes = tiles * count
    chosen = (partner[:, None] == jnp.arange(nodes)).astype(jnp.bfloat16)
    weights = np.zeros((8, length), np.float32)
    weights[0] = 1.0
    weights[1] = offsets_of(length)
    lanes = np.arange(columns)
    sources = jnp.asarray(np.where(lanes < count, np.arange(tiles)[:, None] * count + lanes, -1))
    links = jnp.pad(links, ((0, 0), (0, columns - count)), constant_values=nodes)
    counts = sum(sources[:, :, None] == links[k] for k in range(links.shape[0])).astype(jnp.bfloat16)
    rest = jnp.pad(rest, ((0, 0), (0, columns - count)))
    vmem = pl.BlockSpec(memory_space=pltpu.VMEM)
    smem = pl.BlockSpec(memory_space=pltpu.SMEM)
    return pl.pallas_call(
        moments_kernel,
        in_specs=[smem, smem, vmem, vmem, vmem, vmem, vmem, vmem],
        out_specs=vmem,
        out_shape=jax.ShapeDtypeStruct((tiles, 3 * nodes // columns + 4, columns), jnp.bfloat16),
        scratch_shapes=[
            pltpu.VMEM((nodes, rows, length), jnp.bfloat16),
            pltpu.VMEM((nodes, 2 * length), jnp.bfloat16),
            pltpu.VMEM((nodes, length), jnp.float32),
        ],
        compiler_params=call_params(),
        cost_estimate=pl.CostEstimate(
            flops=nodes * rows * 4 * 2 * length**2, bytes_accessed=2 * lines.size, transcendentals=0
        ),
        name="moments",
    )(partner, place[None], lines, chosen, both, jnp.asarray(weights), counts, rest)


def exchange(x):
    return lax.all_to_all(x, "tile", split_axis=0, concat_axis=0, tiled=True)


def per_device(strips, partner_tile, partner_strip, adjacency, start_positions):
    tiles = lax.axis_size("tile")
    tile_index = lax.axis_index("tile")
    own = strips[0]
    per_tile, length = own.shape[0], own.shape[1]
    half_strips = per_tile // 2
    tables = half_tables(length)
    both = jnp.concatenate([tables[1][:length], tables[1][length:]], 1)
    partner = partner_tile[0] * per_tile + partner_strip[0]
    place = tile_index * per_tile
    links = adjacency[:, 0, :]
    start = start_positions[:, 0, :]

    rows = 2 * length // tiles
    order = np.arange(length).reshape(2, tiles // 2, rows // 2).transpose(1, 0, 2).reshape(-1)
    line_table = tables[0].T[order]
    lines = exchange(lines_of(own, start, line_table, tiles))

    near_low = shifted(own[:half_strips], "sec", -1)
    back_high = shifted(own[half_strips:], "sec", 1)
    strips_here, near_low, back_high = lax.optimization_barrier((own, near_low, back_high))
    fields = spectra_of(strips_here, tables)
    low = flows_of(pair_sums(near_low, fields, 0, True, tables))
    high = flows_of(pair_sums(back_high, fields, half_strips, False, tables))
    depth_out = jnp.concatenate([low, shifted(high, "sec", -1)], 1)

    def mine(values):
        return lax.dynamic_slice_in_dim(values, place, per_tile, 1)

    links = jnp.concatenate([links, mine(partner[None])], 0)
    number = links.shape[0]
    near = shifted(start, "sec", -1)
    rest = start + relax_rate * ((near - start) - number * start + depth_out)

    shares = exchange(moments_of(lines, partner, place, links, rest, both))
    everyone = finish(shares, tiles * per_tile)
    plane_all, current = everyone[:2], everyone[2:]

    plane_out, here = mine(plane_all), mine(current)
    linked = jnp.sum(current[:, links], axis=1)
    near = shifted(here, "sec", -1)
    here = here + relax_rate * (
        (linked - number * here) + (near - here) + plane_out + depth_out
    )
    return (plane_out[:, None, :], depth_out[:, None, :], here[:, None, :])


def solution(mesh):
    return jax.shard_map(
        per_device,
        mesh=mesh,
        in_specs=(
            P("sec", "tile", None, None),
            P("sec", None),
            P("sec", None),
            P(None, "sec", "tile"),
            P(None, "sec", "tile"),
        ),
        out_specs=(P(None, "sec", "tile"), P(None, "sec", "tile"), P(None, "sec", "tile")),
        check_vma=False,
    )
```

```python
import functools
import math

import jax
import jax.numpy as jnp
import numpy as np
from jax import lax
from jax.experimental import pallas as pl
from jax.experimental.pallas import tpu as pltpu
from jax.sharding import PartitionSpec as P

epsilon = 1e-06
relax_rate = 0.1


def shifted(x, axis, by):
    devices = lax.axis_size(axis)
    return lax.ppermute(x, axis, [(i, (i + by) % devices) for i in range(devices)])


def offsets_of(length):
    return ((np.arange(length) + length // 2) % length - length // 2).astype(np.float32)


def angles_of(length):
    indices = np.arange(length)
    return (indices[:, None] * indices[None, :] % length) * (2.0 * math.pi / length)


def half_tables(length):
    half = length // 2
    cosine, sine = np.cos(angles_of(length)), np.sin(angles_of(length))
    to_half = np.concatenate([cosine[:, :half], -sine[:, :half]], 1)
    to_half[:, half] = cosine[:, half]
    from_half = np.concatenate([2.0 * cosine[:half], -2.0 * sine[:half]], 0)
    from_half[0] = 1.0
    from_half[half] = cosine[half]
    both = np.concatenate([cosine, sine], 0)
    return tuple(jnp.asarray(table, jnp.bfloat16) for table in (to_half, both, from_half))


def dot(left, right):
    return jnp.dot(left, right, preferred_element_type=jnp.float32)


def mixed_by(both, halves):
    length, half = both.shape[1], both.shape[1] // 2
    mixed = dot(both, halves)
    return (
        mixed[:length, :half],
        mixed[:length, half:],
        mixed[length:, :half],
        mixed[length:, half:],
    )


def fields_of(images, to_half, both):
    rows = [dot(image, to_half).astype(jnp.bfloat16) for image in images]
    parts = [mixed_by(both, row) for row in rows]
    fields = []
    for cos_re, cos_im, sin_re, sin_im in parts:
        first = lax.broadcasted_iota(jnp.int32, cos_re.shape, 1) == 0
        fields.append(
            tuple(
                field.astype(jnp.bfloat16)
                for field in (
                    jnp.where(first, cos_re, cos_re + sin_im),
                    jnp.where(first, sin_re, sin_re - cos_im),
                    jnp.where(first, cos_im, 0.0),
                    jnp.where(first, sin_im, 0.0),
                )
            )
        )
    return fields


def cross_of(a, b):
    a = [field.astype(jnp.float32) for field in a]
    b = [field.astype(jnp.float32) for field in b]
    real = a[0] * b[0] + a[1] * b[1] + a[2] * b[3] - a[3] * b[2]
    imag = a[1] * b[0] - a[0] * b[1] + a[2] * b[2] + a[3] * b[3]
    return jnp.concatenate([real.astype(jnp.bfloat16), imag.astype(jnp.bfloat16)], 1)


def store_sums(pairs, both, from_half, offsets, out_ref):
    crosses = [cross_of(first, second) for first, second in pairs]
    parts = [mixed_by(both, cross) for cross in crosses]
    uppers = [
        jnp.concatenate(
            [(cos_re - sin_im).astype(jnp.bfloat16), (sin_re + cos_im).astype(jnp.bfloat16)], 1
        )
        for cos_re, cos_im, sin_re, sin_im in parts
    ]
    for k, upper in enumerate(uppers):
        surface = dot(upper, from_half)
        weights = surface * surface
        out_ref[k, 0:1, :] = jnp.sum(weights, axis=0, keepdims=True)
        out_ref[k, 1:2, :] = jnp.sum(weights * offsets, axis=0, keepdims=True)


def split_fields(packed):
    half = packed.shape[-1] // 2
    return packed[0, :, :half], packed[0, :, half:], packed[1, :, :half], packed[1, :, half:]


def spectra_kernel(images_ref, to_half_ref, both_ref, out_ref):
    count = images_ref.shape[0]
    images = [images_ref[k] for k in range(count)]
    for k, (a, b, c, d) in enumerate(fields_of(images, to_half_ref[...], both_ref[...])):
        out_ref[k, 0] = jnp.concatenate([a, b], 1)
        out_ref[k, 1] = jnp.concatenate([c, d], 1)


def pair_kernel(
    other_first, images_ref, fields_ref, to_half_ref, both_ref, from_half_ref, offsets_ref, out_ref
):
    count = fields_ref.shape[0]
    images = [images_ref[k] for k in range(count)]
    others = fields_of(images, to_half_ref[...], both_ref[...])
    owns = [split_fields(fields_ref[k]) for k in range(count)]
    pairs = [(x, y) if other_first else (y, x) for x, y in zip(others, owns)]
    store_sums(pairs, both_ref[...], from_half_ref[...], offsets_ref[...], out_ref)


def whole(table):
    return pl.BlockSpec(table.shape, lambda i: (0,) * table.ndim)


def call_params(megabytes=32):
    return pltpu.CompilerParams(vmem_limit_bytes=megabytes * 1024 * 1024)


def spectra_of(images, tables, batch=4):
    count, length = images.shape[0], images.shape[-1]
    to_half, both, _ = tables
    return pl.pallas_call(
        spectra_kernel,
        grid=(count // batch,),
        in_specs=[
            pl.BlockSpec((batch, length, length), lambda i: (i, 0, 0)),
            whole(to_half),
            whole(both),
        ],
        out_specs=pl.BlockSpec((batch, 2, length, length), lambda i: (i, 0, 0, 0)),
        out_shape=jax.ShapeDtypeStruct((count, 2, length, length), jnp.bfloat16),
        compiler_params=call_params(),
        cost_estimate=pl.CostEstimate(
            flops=count * 6 * length**3, bytes_accessed=count * 6 * length**2, transcendentals=0
        ),
        name="spectra",
    )(images, to_half, both)


def pair_sums(images, fields, start, other_first, tables, batch=4):
    count, length = images.shape[0], images.shape[-1]
    to_half, both, from_half = tables
    spread = jnp.broadcast_to(jnp.asarray(offsets_of(length))[:, None], (length, length))
    return pl.pallas_call(
        functools.partial(pair_kernel, other_first),
        grid=(count // batch,),
        in_specs=[
            pl.BlockSpec((batch, length, length), lambda i: (i, 0, 0)),
            pl.BlockSpec((batch, 2, length, length), lambda i: (i + start // batch, 0, 0, 0)),
            whole(to_half),
            whole(both),
            whole(from_half),
            whole(spread),
        ],
        out_specs=pl.BlockSpec((batch, 8, length), lambda i: (i, 0, 0)),
        out_shape=jax.ShapeDtypeStruct((count, 8, length), jnp.float32),
        compiler_params=call_params(),
        cost_estimate=pl.CostEstimate(
            flops=count * 12 * length**3, bytes_accessed=count * 6 * length**2, transcendentals=0
        ),
        name="pair_sums",
    )(images, fields, to_half, both, from_half, spread)


def flows_of(sums):
    length = sums.shape[-1]
    cells = float(length * length)
    total = jnp.sum(sums[:, 0], axis=1) / cells + epsilon
    along_rows = jnp.sum(sums[:, 1], axis=1) / cells / total
    along_cols = jnp.sum(sums[:, 0] * offsets_of(length), axis=1) / cells / total
    return jnp.stack([along_rows, along_cols], 0)


def lines_kernel(
    images_ref, start_ref, table_ref, out_ref, held, lines, note, read_sems, write_sems
):
    devices, slots, rows, columns = out_ref.shape
    count = slots // 2
    chunks = read_sems.shape[0]
    batch = count // chunks

    def read(chunk):
        strips = pl.ds(chunk * batch, batch)
        return pltpu.make_async_copy(images_ref.at[strips], held.at[strips], read_sems.at[chunk])

    for chunk in range(chunks):
        read(chunk).start()

    height, nodes = start_ref.shape
    note[...] = jnp.zeros_like(note)
    rest = start_ref[...]
    for part in range(3):
        rounded = rest.astype(jnp.bfloat16).astype(jnp.float32)
        note[part * height : (part + 1) * height, :nodes] = rounded
        rest = rest - rounded
    packed = note[...].astype(jnp.bfloat16)
    for device in range(devices):
        lines[device, 2 * count] = packed

    writes = []

    def write(first, number):
        part = pl.ds(first, number)
        copy = pltpu.make_async_copy(
            lines.at[:, part], out_ref.at[:, part], write_sems.at[len(writes)]
        )
        copy.start()
        writes.append(copy)

    write(2 * count, 1)
    table = table_ref[...]
    for chunk in range(chunks):
        read(chunk).wait()
        for strip in range(chunk * batch, (chunk + 1) * batch):
            image = held[strip]
            across = lax.dot_general(
                table, image, (((1,), (1,)), ((), ())), preferred_element_type=jnp.float32
            )
            down = dot(table, image)
            for core, values in enumerate((across, down)):
                values = values.astype(jnp.bfloat16)
                for chip in range(devices // 2):
                    piece = values[chip * rows : (chip + 1) * rows]
                    lines[2 * chip + core, strip] = piece[:, :columns]
                    lines[2 * chip + core, count + strip] = piece[:, columns:]
        write(chunk * batch, batch)
        write(count + chunk * batch, batch)
    for copy in writes:
        copy.wait()


def lines_of(images, start, table, devices, chunks=4):
    count, length = images.shape[0], images.shape[-1]
    rows = 2 * length // devices
    shape = (devices, 2 * count + 1, rows, length // 2)
    vmem = pl.BlockSpec(memory_space=pltpu.VMEM)
    return pl.pallas_call(
        lines_kernel,
        in_specs=[pl.BlockSpec(memory_space=pl.ANY), vmem, vmem],
        out_specs=pl.BlockSpec(memory_space=pl.ANY),
        out_shape=jax.ShapeDtypeStruct(shape, jnp.bfloat16),
        scratch_shapes=[
            pltpu.VMEM(images.shape, images.dtype),
            pltpu.VMEM(shape, jnp.bfloat16),
            pltpu.VMEM((rows, length // 2), jnp.float32),
            pltpu.SemaphoreType.DMA((chunks,)),
            pltpu.SemaphoreType.DMA((2 * chunks + 1,)),
        ],
        compiler_params=call_params(60),
        cost_estimate=pl.CostEstimate(
            flops=count * 4 * length**3, bytes_accessed=count * 6 * length**2, transcendentals=0
        ),
        name="lines",
    )(images, start, table)


def moments_kernel(
    partner_ref, place_ref, lines_ref, chosen_ref, both_ref, weights_ref, counts_ref, rest_ref, out_ref,
    spectra, extra, profile,
):
    tiles, slots, rows, columns = lines_ref.shape
    count, length = slots // 2, 2 * columns
    half = rows // 2
    unroll = math.gcd(tiles, 16)
    both = both_ref[...]
    place = place_ref[0]
    on_first = (place < 2 * count).astype(jnp.int32)
    special = (lax.broadcasted_iota(jnp.int32, (half, length), 0) == 0) & (on_first == 1)
    plain = jnp.where(special, 0.0, 1.0)
    scale = jnp.where(special, 1.0, 2.0)

    def transform(tile):
        lines = jnp.concatenate(
            [lines_ref[tile, :count], lines_ref[tile, count : 2 * count]], 2
        )
        mixed = dot(lines.reshape(count * rows, length), both)
        mixed = mixed.reshape(count, rows, 2 * length)
        cos_re, sin_re = mixed[:, :half, :length], mixed[:, :half, length:]
        cos_im, sin_im = mixed[:, half:, :length], mixed[:, half:, length:]
        fields = jnp.concatenate([cos_re + sin_im * plain, sin_re - cos_im * plain], 1)
        at = pl.multiple_of(tile * count, count)
        spectra[pl.ds(at, count)] = fields.astype(jnp.bfloat16)
        extra[pl.ds(at, count), :] = mixed[:, half, :].astype(jnp.bfloat16)

    @pl.loop(0, tiles // unroll)
    def _(step):
        for k in range(unroll):
            transform(step * unroll + k)

    def surfaces(tile):
        at = tile * count
        first = jnp.stack([spectra[partner_ref[at + k]] for k in range(count)], 0)
        first = first.astype(jnp.float32)
        second = spectra[pl.ds(at, count)].astype(jnp.float32)
        a, b = first[:, :half], first[:, half:]
        c, d = second[:, :half], second[:, half:]
        cross = jnp.concatenate([a * c + b * d, b * c - a * d], 1).astype(jnp.bfloat16)
        mixed = dot(cross.reshape(count * rows, length), both).reshape(count, rows, 2 * length)
        real = mixed[:, :half, :length] - mixed[:, half:, length:]
        imag = mixed[:, :half, length:] + mixed[:, half:, :length]
        profile[pl.ds(at, count), :] = jnp.sum((real * real + imag * imag) * scale, axis=1)

    for tile in range(tiles):
        surfaces(tile)

    second = extra[...]
    first = dot(chosen_ref[...], second)
    second = second.astype(jnp.float32)
    a, b = first[:, :length], first[:, length:]
    c, d = second[:, :length], second[:, length:]
    real = dot((a * c + b * d).astype(jnp.bfloat16), both[:, :length])
    imag = dot((b * c - a * d).astype(jnp.bfloat16), both[:, length:])
    last = real - imag
    profile[...] += last * last * on_first.astype(jnp.float32)
    sums = jnp.zeros((weights_ref.shape[0], tiles * count), jnp.float32)
    rest = profile[...]
    for _ in range(3):
        part = rest.astype(jnp.bfloat16)
        rest = rest - part.astype(jnp.float32)
        sums += lax.dot_general(
            weights_ref[...], part, (((1,), (1,)), ((), ())), preferred_element_type=jnp.float32
        )
    notes = jnp.concatenate([lines_ref[tile, 2 * count] for tile in range(tiles)], 1)
    linked = dot(notes, counts_ref[...])
    linked = (linked[4:6] + linked[2:4]) + linked[0:2]
    base = rest_ref[...] + relax_rate * linked
    width = count
    while width < columns:
        base += pltpu.roll(base, width, 1)
        width *= 2

    def folded(row):
        return jnp.concatenate(
            [sums[row : row + 1, at : at + columns] for at in range(0, tiles * count, columns)], 0
        )

    packed = jnp.concatenate([folded(0), *two_parts(folded(1)), *two_parts(base)], 0)
    packed = packed.astype(jnp.bfloat16)
    for tile in range(tiles):
        out_ref[tile] = packed


def two_parts(values):
    high = values.astype(jnp.bfloat16).astype(jnp.float32)
    return high, values - high


def finish_kernel(shares_ref, out_ref):
    tiles, _, columns = shares_ref.shape
    nodes = out_ref.shape[1]
    folds = nodes // columns
    count = nodes // tiles
    length = 2 * columns
    shares = [shares_ref[tile].astype(jnp.float32) for tile in range(tiles)]
    owner = lax.broadcasted_iota(jnp.int32, (2, columns), 1) // count
    flows = []
    for core in range(2):
        total = sum(shares[core + 2 :: 2], shares[core])
        moment = total[folds : 2 * folds] + total[2 * folds : 3 * folds]
        flows.append(moment / length / (total[:folds] / length + epsilon))
    first = 3 * folds
    for fold in range(folds):
        at = pl.ds(fold * columns, columns)
        base = jnp.zeros((2, columns), jnp.float32)
        for k in range(columns // count):
            share = shares[fold * (columns // count) + k]
            position = share[first : first + 2] + share[first + 2 : first + 4]
            base += jnp.where(owner == k, position, 0.0)
        flow = jnp.concatenate([part[fold : fold + 1] for part in flows], 0)
        out_ref[0:2, at] = flow
        out_ref[2:4, at] = base + relax_rate * flow


def finish(shares, nodes):
    return pl.pallas_call(
        finish_kernel,
        out_shape=jax.ShapeDtypeStruct((4, nodes), jnp.float32),
        compiler_params=call_params(),
        name="finish",
    )(shares)


def moments_of(lines, partner, place, links, rest, both):
    tiles, slots, rows, columns = lines.shape
    count, length = slots // 2, 2 * columns
    nodes = tiles * count
    chosen = (partner[:, None] == jnp.arange(nodes)).astype(jnp.bfloat16)
    weights = np.zeros((16, length), np.float32)
    weights[0] = 1.0
    weights[1] = offsets_of(length)
    lanes = np.arange(columns)
    sources = jnp.asarray(np.where(lanes < count, np.arange(tiles)[:, None] * count + lanes, -1))
    links = jnp.pad(links, ((0, 0), (0, columns - count)), constant_values=nodes)
    sources = sources.reshape(-1, 1)
    counts = sum(sources == links[k] for k in range(links.shape[0])).astype(jnp.bfloat16)
    rest = jnp.pad(rest, ((0, 0), (0, columns - count)))
    vmem = pl.BlockSpec(memory_space=pltpu.VMEM)
    smem = pl.BlockSpec(memory_space=pltpu.SMEM)
    return pl.pallas_call(
        moments_kernel,
        in_specs=[smem, smem, vmem, vmem, vmem, vmem, vmem, vmem],
        out_specs=vmem,
        out_shape=jax.ShapeDtypeStruct((tiles, 3 * nodes // columns + 4, columns), jnp.bfloat16),
        scratch_shapes=[
            pltpu.VMEM((nodes, rows, length), jnp.bfloat16),
            pltpu.VMEM((nodes, 2 * length), jnp.bfloat16),
            pltpu.VMEM((nodes, length), jnp.float32),
        ],
        compiler_params=call_params(),
        cost_estimate=pl.CostEstimate(
            flops=nodes * rows * 4 * 2 * length**2, bytes_accessed=2 * lines.size, transcendentals=0
        ),
        name="moments",
    )(partner, place[None], lines, chosen, both, jnp.asarray(weights, jnp.bfloat16), counts, rest)


def exchange(x):
    return lax.all_to_all(x, "tile", split_axis=0, concat_axis=0, tiled=True)


def per_device(strips, partner_tile, partner_strip, adjacency, start_positions):
    tiles = lax.axis_size("tile")
    tile_index = lax.axis_index("tile")
    own = strips[0]
    per_tile, length = own.shape[0], own.shape[1]
    half_strips = per_tile // 2
    tables = half_tables(length)
    both = jnp.concatenate([tables[1][:length], tables[1][length:]], 1)
    partner = partner_tile[0] * per_tile + partner_strip[0]
    place = tile_index * per_tile
    links = adjacency[:, 0, :]
    start = start_positions[:, 0, :]

    rows = 2 * length // tiles
    order = np.arange(length).reshape(2, tiles // 2, rows // 2).transpose(1, 0, 2).reshape(-1)
    line_table = tables[0].T[order]
    lines = exchange(lines_of(own, start, line_table, tiles))

    near_low = shifted(own[:half_strips], "sec", -1)
    back_high = shifted(own[half_strips:], "sec", 1)
    strips_here, near_low, back_high = lax.optimization_barrier((own, near_low, back_high))
    fields = spectra_of(strips_here, tables)
    low = flows_of(pair_sums(near_low, fields, 0, True, tables))
    high = flows_of(pair_sums(back_high, fields, half_strips, False, tables))
    depth_out = jnp.concatenate([low, shifted(high, "sec", -1)], 1)

    def mine(values):
        return lax.dynamic_slice_in_dim(values, place, per_tile, 1)

    links = jnp.concatenate([links, mine(partner[None])], 0)
    number = links.shape[0]
    near = shifted(start, "sec", -1)
    rest = start + relax_rate * ((near - start) - number * start + depth_out)

    shares = exchange(moments_of(lines, partner, place, links, rest, both))
    everyone = finish(shares, tiles * per_tile)
    plane_all, current = everyone[:2], everyone[2:]

    plane_out, here = mine(plane_all), mine(current)
    linked = jnp.sum(current[:, links], axis=1)
    near = shifted(here, "sec", -1)
    here = here + relax_rate * (
        (linked - number * here) + (near - here) + plane_out + depth_out
    )
    return (plane_out[:, None, :], depth_out[:, None, :], here[:, None, :])


def solution(mesh):
    return jax.shard_map(
        per_device,
        mesh=mesh,
        in_specs=(
            P("sec", "tile", None, None),
            P("sec", None),
            P("sec", None),
            P(None, "sec", "tile"),
            P(None, "sec", "tile"),
        ),
        out_specs=(P(None, "sec", "tile"), P(None, "sec", "tile"), P(None, "sec", "tile")),
        check_vma=False,
    )
```

```python
import functools
import math

import jax
import jax.numpy as jnp
import numpy as np
from jax import lax
from jax.experimental import pallas as pl
from jax.experimental.pallas import tpu as pltpu
from jax.sharding import PartitionSpec as P

epsilon = 1e-06
relax_rate = 0.1


def shifted(x, axis, by):
    devices = lax.axis_size(axis)
    return lax.ppermute(x, axis, [(i, (i + by) % devices) for i in range(devices)])


def offsets_of(length):
    return ((np.arange(length) + length // 2) % length - length // 2).astype(np.float32)


def angles_of(length):
    indices = np.arange(length)
    return (indices[:, None] * indices[None, :] % length) * (2.0 * math.pi / length)


def half_tables(length):
    half = length // 2
    cosine, sine = np.cos(angles_of(length)), np.sin(angles_of(length))
    to_half = np.concatenate([cosine[:, :half], -sine[:, :half]], 1)
    to_half[:, half] = cosine[:, half]
    from_half = np.concatenate([2.0 * cosine[:half], -2.0 * sine[:half]], 0)
    from_half[0] = 1.0
    from_half[half] = cosine[half]
    both = np.concatenate([cosine, sine], 0)
    return tuple(jnp.asarray(table, jnp.bfloat16) for table in (to_half, both, from_half))


def dot(left, right):
    return jnp.dot(left, right, preferred_element_type=jnp.float32)


def mixed_by(both, halves):
    length, half = both.shape[1], both.shape[1] // 2
    mixed = dot(both, halves)
    return (
        mixed[:length, :half],
        mixed[:length, half:],
        mixed[length:, :half],
        mixed[length:, half:],
    )


def fields_of(images, to_half, both):
    rows = [dot(image, to_half).astype(jnp.bfloat16) for image in images]
    parts = [mixed_by(both, row) for row in rows]
    fields = []
    for cos_re, cos_im, sin_re, sin_im in parts:
        first = lax.broadcasted_iota(jnp.int32, cos_re.shape, 1) == 0
        fields.append(
            tuple(
                field.astype(jnp.bfloat16)
                for field in (
                    jnp.where(first, cos_re, cos_re + sin_im),
                    jnp.where(first, sin_re, sin_re - cos_im),
                    jnp.where(first, cos_im, 0.0),
                    jnp.where(first, sin_im, 0.0),
                )
            )
        )
    return fields


def cross_of(a, b):
    a = [field.astype(jnp.float32) for field in a]
    b = [field.astype(jnp.float32) for field in b]
    real = a[0] * b[0] + a[1] * b[1] + a[2] * b[3] - a[3] * b[2]
    imag = a[1] * b[0] - a[0] * b[1] + a[2] * b[2] + a[3] * b[3]
    return jnp.concatenate([real.astype(jnp.bfloat16), imag.astype(jnp.bfloat16)], 1)


def store_sums(pairs, both, from_half, offsets, out_ref):
    crosses = [cross_of(first, second) for first, second in pairs]
    parts = [mixed_by(both, cross) for cross in crosses]
    uppers = [
        jnp.concatenate(
            [(cos_re - sin_im).astype(jnp.bfloat16), (sin_re + cos_im).astype(jnp.bfloat16)], 1
        )
        for cos_re, cos_im, sin_re, sin_im in parts
    ]
    for k, upper in enumerate(uppers):
        surface = dot(upper, from_half)
        weights = surface * surface
        out_ref[k, 0:1, :] = jnp.sum(weights, axis=0, keepdims=True)
        out_ref[k, 1:2, :] = jnp.sum(weights * offsets, axis=0, keepdims=True)


def split_fields(packed):
    half = packed.shape[-1] // 2
    return packed[0, :, :half], packed[0, :, half:], packed[1, :, :half], packed[1, :, half:]


def spectra_kernel(images_ref, to_half_ref, both_ref, out_ref):
    count = images_ref.shape[0]
    images = [images_ref[k] for k in range(count)]
    for k, (a, b, c, d) in enumerate(fields_of(images, to_half_ref[...], both_ref[...])):
        out_ref[k, 0] = jnp.concatenate([a, b], 1)
        out_ref[k, 1] = jnp.concatenate([c, d], 1)


def pair_kernel(
    other_first, images_ref, fields_ref, to_half_ref, both_ref, from_half_ref, offsets_ref, out_ref
):
    count = fields_ref.shape[0]
    images = [images_ref[k] for k in range(count)]
    others = fields_of(images, to_half_ref[...], both_ref[...])
    owns = [split_fields(fields_ref[k]) for k in range(count)]
    pairs = [(x, y) if other_first else (y, x) for x, y in zip(others, owns)]
    store_sums(pairs, both_ref[...], from_half_ref[...], offsets_ref[...], out_ref)


def whole(table):
    return pl.BlockSpec(table.shape, lambda i: (0,) * table.ndim)


def call_params(megabytes=32):
    return pltpu.CompilerParams(vmem_limit_bytes=megabytes * 1024 * 1024)


def spectra_of(images, tables, batch=4):
    count, length = images.shape[0], images.shape[-1]
    to_half, both, _ = tables
    return pl.pallas_call(
        spectra_kernel,
        grid=(count // batch,),
        in_specs=[
            pl.BlockSpec((batch, length, length), lambda i: (i, 0, 0)),
            whole(to_half),
            whole(both),
        ],
        out_specs=pl.BlockSpec((batch, 2, length, length), lambda i: (i, 0, 0, 0)),
        out_shape=jax.ShapeDtypeStruct((count, 2, length, length), jnp.bfloat16),
        compiler_params=call_params(),
        cost_estimate=pl.CostEstimate(
            flops=count * 6 * length**3, bytes_accessed=count * 6 * length**2, transcendentals=0
        ),
        name="spectra",
    )(images, to_half, both)


def pair_sums(images, fields, start, other_first, tables, batch=4):
    count, length = images.shape[0], images.shape[-1]
    to_half, both, from_half = tables
    spread = jnp.broadcast_to(jnp.asarray(offsets_of(length))[:, None], (length, length))
    return pl.pallas_call(
        functools.partial(pair_kernel, other_first),
        grid=(count // batch,),
        in_specs=[
            pl.BlockSpec((batch, length, length), lambda i: (i, 0, 0)),
            pl.BlockSpec((batch, 2, length, length), lambda i: (i + start // batch, 0, 0, 0)),
            whole(to_half),
            whole(both),
            whole(from_half),
            whole(spread),
        ],
        out_specs=pl.BlockSpec((batch, 8, length), lambda i: (i, 0, 0)),
        out_shape=jax.ShapeDtypeStruct((count, 8, length), jnp.float32),
        compiler_params=call_params(),
        cost_estimate=pl.CostEstimate(
            flops=count * 12 * length**3, bytes_accessed=count * 6 * length**2, transcendentals=0
        ),
        name="pair_sums",
    )(images, fields, to_half, both, from_half, spread)


def flows_of(sums):
    length = sums.shape[-1]
    cells = float(length * length)
    total = jnp.sum(sums[:, 0], axis=1) / cells + epsilon
    along_rows = jnp.sum(sums[:, 1], axis=1) / cells / total
    along_cols = jnp.sum(sums[:, 0] * offsets_of(length), axis=1) / cells / total
    return jnp.stack([along_rows, along_cols], 0)


def lines_kernel(
    images_ref, start_ref, table_ref, out_ref, held, lines, note, read_sems, write_sems
):
    devices, slots, rows, columns = out_ref.shape
    count = slots // 2
    chunks = read_sems.shape[0]
    batch = count // chunks

    def read(chunk):
        strips = pl.ds(chunk * batch, batch)
        return pltpu.make_async_copy(images_ref.at[strips], held.at[strips], read_sems.at[chunk])

    for chunk in range(chunks):
        read(chunk).start()

    height, nodes = start_ref.shape
    note[...] = jnp.zeros_like(note)
    rest = start_ref[...]
    for part in range(3):
        rounded = rest.astype(jnp.bfloat16).astype(jnp.float32)
        note[part * height : (part + 1) * height, :nodes] = rounded
        rest = rest - rounded
    packed = note[...].astype(jnp.bfloat16)
    for device in range(devices):
        lines[device, 2 * count] = packed

    writes = []

    def write(first, number):
        part = pl.ds(first, number)
        copy = pltpu.make_async_copy(
            lines.at[:, part], out_ref.at[:, part], write_sems.at[len(writes)]
        )
        copy.start()
        writes.append(copy)

    write(2 * count, 1)
    table = table_ref[...]
    for chunk in range(chunks):
        read(chunk).wait()
        for strip in range(chunk * batch, (chunk + 1) * batch):
            image = held[strip]
            across = lax.dot_general(
                table, image, (((1,), (1,)), ((), ())), preferred_element_type=jnp.float32
            )
            down = dot(table, image)
            for core, values in enumerate((across, down)):
                values = values.astype(jnp.bfloat16)
                for chip in range(devices // 2):
                    piece = values[chip * rows : (chip + 1) * rows]
                    lines[2 * chip + core, strip] = piece[:, :columns]
                    lines[2 * chip + core, count + strip] = piece[:, columns:]
        write(chunk * batch, batch)
        write(count + chunk * batch, batch)
    for copy in writes:
        copy.wait()


def lines_of(images, start, table, devices, chunks=4):
    count, length = images.shape[0], images.shape[-1]
    rows = 2 * length // devices
    shape = (devices, 2 * count + 1, rows, length // 2)
    vmem = pl.BlockSpec(memory_space=pltpu.VMEM)
    return pl.pallas_call(
        lines_kernel,
        in_specs=[pl.BlockSpec(memory_space=pl.ANY), vmem, vmem],
        out_specs=pl.BlockSpec(memory_space=pl.ANY),
        out_shape=jax.ShapeDtypeStruct(shape, jnp.bfloat16),
        scratch_shapes=[
            pltpu.VMEM(images.shape, images.dtype),
            pltpu.VMEM(shape, jnp.bfloat16),
            pltpu.VMEM((rows, length // 2), jnp.float32),
            pltpu.SemaphoreType.DMA((chunks,)),
            pltpu.SemaphoreType.DMA((2 * chunks + 1,)),
        ],
        compiler_params=call_params(60),
        cost_estimate=pl.CostEstimate(
            flops=count * 4 * length**3, bytes_accessed=count * 6 * length**2, transcendentals=0
        ),
        name="lines",
    )(images, start, table)


def moments_kernel(
    partner_ref, place_ref, lines_ref, chosen_ref, both_ref, weights_ref, counts_ref, rest_ref, out_ref,
    spectra, extra, profile,
):
    tiles, slots, rows, columns = lines_ref.shape
    count, length = slots // 2, 2 * columns
    half = rows // 2
    unroll = math.gcd(tiles, 16)
    both = both_ref[...]
    place = place_ref[0]
    on_first = (place < 2 * count).astype(jnp.int32)
    special = (lax.broadcasted_iota(jnp.int32, (half, length), 0) == 0) & (on_first == 1)
    plain = jnp.where(special, 0.0, 1.0)
    scale = jnp.where(special, 1.0, 2.0)

    def transform(tile):
        lines = jnp.concatenate(
            [lines_ref[tile, :count], lines_ref[tile, count : 2 * count]], 2
        )
        mixed = dot(lines.reshape(count * rows, length), both)
        mixed = mixed.reshape(count, rows, 2 * length)
        cos_re, sin_re = mixed[:, :half, :length], mixed[:, :half, length:]
        cos_im, sin_im = mixed[:, half:, :length], mixed[:, half:, length:]
        fields = jnp.concatenate([cos_re + sin_im * plain, sin_re - cos_im * plain], 1)
        at = pl.multiple_of(tile * count, count)
        spectra[pl.ds(at, count)] = fields.astype(jnp.bfloat16)
        extra[pl.ds(at, count), :] = mixed[:, half, :].astype(jnp.bfloat16)

    @pl.loop(0, tiles // unroll)
    def _(step):
        for k in range(unroll):
            transform(step * unroll + k)

    second = extra[...]
    first = dot(chosen_ref[...], second)
    second = second.astype(jnp.float32)
    a, b = first[:, :length], first[:, length:]
    c, d = second[:, :length], second[:, length:]
    real = dot((a * c + b * d).astype(jnp.bfloat16), both[:, :length])
    imag = dot((b * c - a * d).astype(jnp.bfloat16), both[:, length:])
    last = real - imag
    profile[...] = last * last * on_first.astype(jnp.float32)
    notes = jnp.concatenate([lines_ref[tile, 2 * count] for tile in range(tiles)], 1)
    linked = dot(notes, counts_ref[...])

    def surfaces(tile):
        at = tile * count
        first = jnp.stack([spectra[partner_ref[at + k]] for k in range(count)], 0)
        first = first.astype(jnp.float32)
        second = spectra[pl.ds(at, count)].astype(jnp.float32)
        a, b = first[:, :half], first[:, half:]
        c, d = second[:, :half], second[:, half:]
        cross = jnp.concatenate([a * c + b * d, b * c - a * d], 1).astype(jnp.bfloat16)
        mixed = dot(cross.reshape(count * rows, length), both).reshape(count, rows, 2 * length)
        real = mixed[:, :half, :length] - mixed[:, half:, length:]
        imag = mixed[:, :half, length:] + mixed[:, half:, :length]
        profile[pl.ds(at, count), :] += jnp.sum((real * real + imag * imag) * scale, axis=1)

    for tile in range(tiles):
        surfaces(tile)

    sums = jnp.zeros((weights_ref.shape[0], tiles * count), jnp.float32)
    rest = profile[...]
    for _ in range(3):
        part = rest.astype(jnp.bfloat16)
        rest = rest - part.astype(jnp.float32)
        sums += lax.dot_general(
            weights_ref[...], part, (((1,), (1,)), ((), ())), preferred_element_type=jnp.float32
        )
    linked = (linked[4:6] + linked[2:4]) + linked[0:2]
    base = rest_ref[...] + relax_rate * linked
    width = count
    while width < columns:
        base += pltpu.roll(base, width, 1)
        width *= 2

    def folded(row):
        return jnp.concatenate(
            [sums[row : row + 1, at : at + columns] for at in range(0, tiles * count, columns)], 0
        )

    packed = jnp.concatenate([folded(0), *two_parts(folded(1)), *two_parts(base)], 0)
    packed = packed.astype(jnp.bfloat16)
    for tile in range(tiles):
        out_ref[tile] = packed


def two_parts(values):
    high = values.astype(jnp.bfloat16).astype(jnp.float32)
    return high, values - high


def finish_kernel(shares_ref, out_ref):
    tiles, _, columns = shares_ref.shape
    nodes = out_ref.shape[1]
    folds = nodes // columns
    count = nodes // tiles
    length = 2 * columns
    shares = [shares_ref[tile].astype(jnp.float32) for tile in range(tiles)]
    owner = lax.broadcasted_iota(jnp.int32, (2, columns), 1) // count
    flows = []
    for core in range(2):
        total = sum(shares[core + 2 :: 2], shares[core])
        moment = total[folds : 2 * folds] + total[2 * folds : 3 * folds]
        flows.append(moment / length / (total[:folds] / length + epsilon))
    first = 3 * folds
    for fold in range(folds):
        at = pl.ds(fold * columns, columns)
        base = jnp.zeros((2, columns), jnp.float32)
        for k in range(columns // count):
            share = shares[fold * (columns // count) + k]
            position = share[first : first + 2] + share[first + 2 : first + 4]
            base += jnp.where(owner == k, position, 0.0)
        flow = jnp.concatenate([part[fold : fold + 1] for part in flows], 0)
        out_ref[0:2, at] = flow
        out_ref[2:4, at] = base + relax_rate * flow


def finish(shares, nodes):
    return pl.pallas_call(
        finish_kernel,
        out_shape=jax.ShapeDtypeStruct((4, nodes), jnp.float32),
        compiler_params=call_params(),
        name="finish",
    )(shares)


def moments_of(lines, partner, place, links, rest, both):
    tiles, slots, rows, columns = lines.shape
    count, length = slots // 2, 2 * columns
    nodes = tiles * count
    chosen = (partner[:, None] == jnp.arange(nodes)).astype(jnp.bfloat16)
    weights = np.zeros((16, length), np.float32)
    weights[0] = 1.0
    weights[1] = offsets_of(length)
    lanes = np.arange(columns)
    sources = jnp.asarray(np.where(lanes < count, np.arange(tiles)[:, None] * count + lanes, -1))
    links = jnp.pad(links, ((0, 0), (0, columns - count)), constant_values=nodes)
    sources = sources.reshape(-1, 1)
    counts = sum(sources == links[k] for k in range(links.shape[0])).astype(jnp.bfloat16)
    rest = jnp.pad(rest, ((0, 0), (0, columns - count)))
    vmem = pl.BlockSpec(memory_space=pltpu.VMEM)
    smem = pl.BlockSpec(memory_space=pltpu.SMEM)
    return pl.pallas_call(
        moments_kernel,
        in_specs=[smem, smem, vmem, vmem, vmem, vmem, vmem, vmem],
        out_specs=vmem,
        out_shape=jax.ShapeDtypeStruct((tiles, 3 * nodes // columns + 4, columns), jnp.bfloat16),
        scratch_shapes=[
            pltpu.VMEM((nodes, rows, length), jnp.bfloat16),
            pltpu.VMEM((nodes, 2 * length), jnp.bfloat16),
            pltpu.VMEM((nodes, length), jnp.float32),
        ],
        compiler_params=call_params(),
        cost_estimate=pl.CostEstimate(
            flops=nodes * rows * 4 * 2 * length**2, bytes_accessed=2 * lines.size, transcendentals=0
        ),
        name="moments",
    )(partner, place[None], lines, chosen, both, jnp.asarray(weights, jnp.bfloat16), counts, rest)


def exchange(x):
    return lax.all_to_all(x, "tile", split_axis=0, concat_axis=0, tiled=True)


def per_device(strips, partner_tile, partner_strip, adjacency, start_positions):
    tiles = lax.axis_size("tile")
    tile_index = lax.axis_index("tile")
    own = strips[0]
    per_tile, length = own.shape[0], own.shape[1]
    half_strips = per_tile // 2
    tables = half_tables(length)
    both = jnp.concatenate([tables[1][:length], tables[1][length:]], 1)
    partner = partner_tile[0] * per_tile + partner_strip[0]
    place = tile_index * per_tile
    links = adjacency[:, 0, :]
    start = start_positions[:, 0, :]

    rows = 2 * length // tiles
    order = np.arange(length).reshape(2, tiles // 2, rows // 2).transpose(1, 0, 2).reshape(-1)
    line_table = tables[0].T[order]
    lines = exchange(lines_of(own, start, line_table, tiles))

    near_low = shifted(own[:half_strips], "sec", -1)
    back_high = shifted(own[half_strips:], "sec", 1)
    strips_here, near_low, back_high = lax.optimization_barrier((own, near_low, back_high))
    fields = spectra_of(strips_here, tables)
    low = flows_of(pair_sums(near_low, fields, 0, True, tables))
    high = flows_of(pair_sums(back_high, fields, half_strips, False, tables))
    depth_out = jnp.concatenate([low, shifted(high, "sec", -1)], 1)

    def mine(values):
        return lax.dynamic_slice_in_dim(values, place, per_tile, 1)

    links = jnp.concatenate([links, mine(partner[None])], 0)
    number = links.shape[0]
    near = shifted(start, "sec", -1)
    rest = start + relax_rate * ((near - start) - number * start + depth_out)

    shares = exchange(moments_of(lines, partner, place, links, rest, both))
    everyone = finish(shares, tiles * per_tile)
    plane_all, current = everyone[:2], everyone[2:]

    plane_out, here = mine(plane_all), mine(current)
    linked = jnp.sum(current[:, links], axis=1)
    near = shifted(here, "sec", -1)
    here = here + relax_rate * (
        (linked - number * here) + (near - here) + plane_out + depth_out
    )
    return (plane_out[:, None, :], depth_out[:, None, :], here[:, None, :])


def solution(mesh):
    return jax.shard_map(
        per_device,
        mesh=mesh,
        in_specs=(
            P("sec", "tile", None, None),
            P("sec", None),
            P("sec", None),
            P(None, "sec", "tile"),
            P(None, "sec", "tile"),
        ),
        out_specs=(P(None, "sec", "tile"), P(None, "sec", "tile"), P(None, "sec", "tile")),
        check_vma=False,
    )
```
